256 devices in a mesh: dp: 4 (over y), seq: 64 (over x, z, core).
Axes of the slice: x: 4, y: 4, z: 8, core: 2. Of those that a mesh axis runs over, the one named last changes fastest.
Arguments:
- grid_fields: bfloat16 [4, 100, 262144], P('dp', None, 'seq'), may hold values from -6 to 6
- mesh_latent: bfloat16 [16384, 1024], P('seq'), may hold values from -6 to 6
- edge_source: int32 [64, 64, 128], P('seq'), may hold values from 0 to 4095
- edge_target: int32 [64, 64, 128], P('seq'), may hold values from 0 to 255, as said below
- edge_count: int32 [64, 64], replicated, may hold values from 0 to 128, as said below
- edge_bias: float32 [64, 64, 128], P('seq'), may hold values from -6 to 300
- encoder_proj: bfloat16 [100, 2048], replicated, may hold values from -0.625 to 0.625
- norm_gain: float32 [1024], replicated, may hold values from 0.5 to 1.5
- processor_proj: bfloat16 [1024, 3072], replicated, may hold values from -0.1875 to 0.1875
- offset_bias: float32 [16, 257], replicated, may hold values from -6 to 300
- windows: int32 [16], replicated, may hold values from 4 to 128, as said below
- output_proj: bfloat16 [1024, 1024], replicated, may hold values from -0.1875 to 0.1875
- cotangent: bfloat16 [4, 16384, 1024], P('dp', 'seq'), may hold values from -6 to 6
Outputs:
- processed: bfloat16 [4, 16384, 1024], P('dp', 'seq')
- output_grad: float32 [1024, 1024], P('seq')
The draws below stay inside these ranges and needn't reach their ends.
Inputs may be any that keep to these rules, and one draw needn't show every extreme that they name: `edge_target`: slots 2m and 2m + 1 of a block name the same row. `edge_count`: in every draw one owner receives 128 live slots from every source device. `windows`: some head's reach is exactly 128.
All inputs are finite; a program needn't handle non-finite values.
Results may differ from the reference program's by a relative error of at most 0.02.
Values may be sent and summed in bfloat16 or wider, within the bound.
A program may use at most 192 MiB of HBM per device.

```python
import math
import jax
import jax.numpy as jnp
from jax import lax

D = 1024
HEADS = 16
CH = 100
HALF = 128
MESH_DEV = 256
SHARDS = 64
SAMPLES = 4
GRID_DEV = 4096
CAP = 128
MESH = 16384
GRID = 262144


def draw_edge_target(key, part):
    key = jax.random.fold_in(key, 11)
    paired = jax.random.randint(key, (SHARDS, SHARDS, CAP // 2), 0, MESH_DEV)
    return jnp.repeat(paired, 2, axis=2).astype(jnp.int32)


def draw_edge_count(key, part):
    key = jax.random.fold_in(key, 23)
    first_key, second_key, third_key = jax.random.split(key, 3)
    levels = jax.random.randint(first_key, (SHARDS,), 1, 5)
    drawn = jax.random.randint(second_key, (SHARDS, SHARDS), 0, CAP + 1)
    counts = drawn * levels[None, :] // 4
    full_owner = jax.random.randint(third_key, (), 0, SHARDS)
    owners = jnp.arange(SHARDS)[None, :]
    return jnp.where(owners == full_owner, CAP, counts).astype(jnp.int32)


def draw_edge_bias(key, part):
    key = jax.random.fold_in(key, 37)
    keys = jax.random.split(key, 1)
    shape = (SHARDS, SHARDS, CAP)
    return jnp.clip(jax.random.normal(keys[0], shape, jnp.float32), -6.0, 6.0)


def draw_offset_bias(key, part):
    key = jax.random.fold_in(key, 53)
    keys = jax.random.split(key, 1)
    shape = (HEADS, 2 * HALF + 1)
    return jnp.clip(jax.random.normal(keys[0], shape, jnp.float32), -6.0, 6.0)


def draw_windows(key, part):
    key = jax.random.fold_in(key, 71)
    first_key, second_key = jax.random.split(key)
    reaches = jax.random.randint(first_key, (HEADS,), 4, HALF + 1)
    widest = jax.random.randint(second_key, (), 0, HEADS)
    return jnp.where(jnp.arange(HEADS) == widest, HALF, reaches).astype(jnp.int32)


def set_ends(entries, key, least, high):
    longest = entries.shape.index(max(entries.shape))
    spots = []
    for shift in (0, 1):
        where = [jax.random.randint(jax.random.fold_in(key, axis), (), 0, length) for axis, length in enumerate(entries.shape)]
        where[longest] = (where[longest] + shift) % entries.shape[longest]
        spots.append(tuple(where))
    return entries.at[spots[0]].set(least).at[spots[1]].set(high)


def shard_levels(stream_key, shape, pieces, low, top_value):
    loudness, own = 1.0, jax.random.fold_in(stream_key, 6)
    for axis_at, shards_of in pieces:
        heights = jnp.exp(jax.random.uniform(jax.random.fold_in(own, axis_at), (shards_of,), jnp.float32, low / len(pieces), top_value / len(pieces)))
        loudness = loudness * jnp.repeat(heights, shape[axis_at] // shards_of).reshape([-1 if axis == axis_at else 1 for axis in range(len(shape))])
    return loudness


def normal_values(stream_key, dims, width, bound, cuts=(), held_as=jnp.bfloat16):
    loudness = shard_levels(stream_key, dims, cuts, -0.22, 0.18) if cuts else 1.0
    result = jax.random.normal(stream_key, dims, jnp.float32) * width * loudness
    return jnp.minimum(jnp.maximum(result, -bound), bound).astype(held_as)


def setup_inputs(seed: int = 0) -> dict:
    splits = jax.random.split(jax.random.key(seed), 14)
    grid_fields = normal_values(splits[0], (SAMPLES, CH, GRID), 1.0, 6.0, ((0, 4), (2, 64)))
    mesh_latent = normal_values(splits[1], (MESH, D), 1.0, 6.0, ((0, 64),))
    edge_source = set_ends(jax.random.randint(splits[2], (SHARDS, SHARDS, CAP), 0, GRID_DEV), jax.random.fold_in(splits[2], 1), 0, GRID_DEV - 1).astype(jnp.int32)
    edge_target = draw_edge_target(jax.random.fold_in(splits[13], 71), 0)
    edge_count = draw_edge_count(jax.random.fold_in(splits[13], 71), 0)
    edge_bias = draw_edge_bias(jax.random.fold_in(splits[13], 71), 0)
    encoder_proj = normal_values(splits[6], (CH, 2 * D), CH ** -0.5, 0.625)
    norm_gain = jnp.clip(1.0 + 0.1 * jax.random.normal(splits[7], (D,), jnp.float32), 0.5, 1.5)
    processor_proj = normal_values(splits[8], (D, 3 * D), D ** -0.5, 0.1875)
    offset_bias = draw_offset_bias(jax.random.fold_in(splits[13], 71), 0)
    windows = draw_windows(jax.random.fold_in(splits[13], 71), 0)
    output_proj = normal_values(splits[11], (D, D), D ** -0.5, 0.1875)
    cotangent = normal_values(splits[12], (SAMPLES, MESH, D), 1.0, 6.0, ((0, 4), (1, 64)))
    return {"grid_fields": grid_fields, "mesh_latent": mesh_latent, "edge_source": edge_source, "edge_target": edge_target, "edge_count": edge_count, "edge_bias": edge_bias, "encoder_proj": encoder_proj, "norm_gain": norm_gain, "processor_proj": processor_proj, "offset_bias": offset_bias, "windows": windows, "output_proj": output_proj, "cotangent": cotangent}


def attend_edges(running, slot_values, targets, slot_bias, is_live, latent, head_count):
    running_max, running_sum, running_acc = running
    node_count, model_width = latent.shape
    head_size = model_width // head_count
    slot_count = targets.shape[0]
    key_part = slot_values[:, :model_width].reshape(slot_count, head_count, head_size)
    value_part = slot_values[:, model_width:].reshape(slot_count, head_count, head_size)
    queries = jnp.take(latent, targets, axis=0).astype(jnp.float32).reshape(slot_count, head_count, head_size)
    scores = lax.optimization_barrier(jnp.sum(queries * key_part, axis=-1)) / math.sqrt(head_size) + slot_bias[:, None]
    scores = jnp.where(is_live[:, None], scores, -1e+30)
    block_max = jax.ops.segment_max(scores, targets, num_segments=node_count)
    new_max = jnp.maximum(running_max, block_max)
    factor = jnp.exp(running_max - new_max)
    weights = jnp.exp(scores - jnp.take(new_max, targets, axis=0))
    running_sum = running_sum * factor + jax.ops.segment_sum(weights, targets, num_segments=node_count)
    running_acc = running_acc * factor[:, :, None] + jax.ops.segment_sum(weights[:, :, None] * value_part, targets, num_segments=node_count)
    return (new_max, running_sum, running_acc)

def layer_norm(state, gain):
    center = state - lax.optimization_barrier(jnp.mean(state, axis=-1, keepdims=True))
    variance = lax.optimization_barrier(jnp.mean(center * center, axis=-1, keepdims=True))
    return (center * lax.rsqrt(variance + 1e-05) * gain).astype(jnp.bfloat16)

def window_attention(queries, extended, offset_bias, windows, first_row, row_total, reach):
    query_count, model_width = queries.shape
    head_count = offset_bias.shape[0]
    head_size = model_width // head_count
    key_count = extended.shape[0]
    query_heads = queries.reshape(query_count, head_count, head_size).astype(jnp.float32)
    key_heads = extended[:, :model_width].reshape(key_count, head_count, head_size).astype(jnp.float32)
    value_heads = extended[:, model_width:].reshape(key_count, head_count, head_size).astype(jnp.float32)
    scores = jnp.einsum('qhd,khd->hqk', query_heads, key_heads) / math.sqrt(head_size)
    offset = jnp.arange(key_count, dtype=jnp.int32)[None, :] - reach - jnp.arange(query_count, dtype=jnp.int32)[:, None]
    key_rows = first_row - reach + jnp.arange(key_count, dtype=jnp.int32)
    inside = (key_rows >= 0) & (key_rows < row_total)
    offset_table = jnp.take(offset_bias, jnp.clip(offset + reach, 0, 2 * reach), axis=1)
    allowed = inside[None, None, :] & (jnp.abs(offset)[None, :, :] <= windows[:, None, None])
    scores = jnp.where(allowed, scores + offset_table, -1e+30)
    peak = lax.optimization_barrier(jnp.max(scores, axis=-1, keepdims=True))
    powered = jnp.exp(scores - peak)
    weights = (powered / lax.optimization_barrier(jnp.sum(powered, axis=-1, keepdims=True))).astype(jnp.bfloat16)
    mixture = jnp.einsum('hqk,khd->qhd', weights.astype(jnp.float32), value_heads)
    return mixture.reshape(query_count, model_width).astype(jnp.bfloat16)

def reference(grid_fields, mesh_latent, edge_source, edge_target, edge_count, edge_bias, encoder_proj, norm_gain, processor_proj, offset_bias, windows, output_proj, cotangent):
    head_size = D // HEADS
    slot_index = jnp.arange(CAP, dtype=jnp.int32)
    owner_start = jnp.arange(SHARDS, dtype=jnp.int32) * MESH_DEV
    outputs = []
    gradient = jnp.zeros((D, D), jnp.float32)
    for sample in range(SAMPLES):
        grid_sample = grid_fields[sample]

        def source_step(running, source):
            source_block = lax.dynamic_slice_in_dim(grid_sample, source * GRID_DEV, GRID_DEV, 1)
            projected = jnp.dot(source_block.T, encoder_proj, preferred_element_type=jnp.float32)
            source_rows = lax.dynamic_index_in_dim(edge_source, source, 0, keepdims=False).reshape(-1)
            slot_values = jnp.take(projected, source_rows, axis=0)
            targets = lax.dynamic_index_in_dim(edge_target, source, 1, keepdims=False) + owner_start[:, None]
            slot_bias = lax.dynamic_index_in_dim(edge_bias, source, 1, keepdims=False).reshape(-1)
            counts = lax.dynamic_index_in_dim(edge_count, source, 0, keepdims=False)
            is_live = (slot_index[None, :] < counts[:, None]).reshape(-1)
            return (attend_edges(running, slot_values, targets.reshape(-1), slot_bias, is_live, mesh_latent, HEADS), None)
        initial = (jnp.zeros((MESH, HEADS), jnp.float32), jnp.ones((MESH, HEADS), jnp.float32), jnp.zeros((MESH, HEADS, head_size), jnp.float32))
        running, unused = lax.scan(source_step, initial, jnp.arange(SHARDS, dtype=jnp.int32))
        encoded = (running[2] / running[1][:, :, None]).reshape(MESH, D)
        hidden_state = mesh_latent.astype(jnp.float32) + encoded
        normalized = layer_norm(hidden_state, norm_gain)
        projected_all = jnp.dot(normalized, processor_proj, preferred_element_type=jnp.float32).astype(jnp.bfloat16)
        queries = projected_all[:, :D]
        padded = jnp.pad(projected_all[:, D:], ((HALF, HALF), (0, 0)))

        def query_block(block):
            first = block * MESH_DEV
            block_queries = lax.dynamic_slice_in_dim(queries, first, MESH_DEV, 0)
            extended = lax.dynamic_slice_in_dim(padded, first, MESH_DEV + 2 * HALF, 0)
            return window_attention(block_queries, extended, offset_bias, windows, first, MESH, HALF)
        attended = lax.map(query_block, jnp.arange(SHARDS, dtype=jnp.int32)).reshape(MESH, D)
        processed = (hidden_state + jnp.dot(attended, output_proj, preferred_element_type=jnp.float32)).astype(jnp.bfloat16)
        outputs.append(processed)
        gradient = gradient + jnp.dot(attended.T, cotangent[sample], preferred_element_type=jnp.float32)
    return (jnp.stack(outputs), gradient)
```

```python
import functools

import jax
import jax.numpy as jnp
from jax import lax
from jax.experimental import pallas as pl
from jax.experimental.pallas import tpu as pltpu
from jax.sharding import PartitionSpec as P

MESH = pl.DeviceIdType.MESH
X, Z, CORES, Y = 4, 8, 2, 4
NEG = -1e30
F32 = jnp.float32
BF16 = jnp.bfloat16
VMEM_LIMIT = 56 * 1024 * 1024

NT = (((1,), (1,)), ((), ()))
TN = (((0,), (0,)), ((), ()))


def vmem():
    return pl.BlockSpec(memory_space=pltpu.VMEM)


def gather_kernel(source_ref, grid_ref, out_ref, table, stage):
    channels = grid_ref.shape[1]
    owners, capacity = source_ref.shape
    stage[...] = jnp.zeros_like(stage)

    def turn(chunk, carry):
        start = pl.multiple_of(chunk * 128, 128)
        stage[0:channels, :] = grid_ref[0, :, pl.ds(start, 128)].astype(F32)
        table[pl.ds(start, 128), :] = stage[...].T
        return carry

    lax.fori_loop(0, grid_ref.shape[2] // 128, turn, 0)

    def owner_step(owner, carry):
        for slot in range(capacity):
            row = (slot % 2) * (capacity // 2) + slot // 2
            stage[row : row + 1, :] = table[pl.ds(source_ref[owner, slot], 1), :]
        out_ref[owner] = stage[...].astype(BF16)
        return carry

    lax.fori_loop(0, owners, owner_step, 0)


def edge_kernel(
    field_ref, target_ref, bias_ref, latent_t_ref, proj_t_ref, latent_ref, gain_ref,
    hidden_ref, norm_ref, acc, peak_ref, total_ref,
):
    step = pl.program_id(0)
    width, rows = latent_t_ref.shape
    heads = peak_ref.shape[0]
    size = width // heads
    sources, capacity, channels = field_ref.shape
    half = capacity // 2
    pairs = sources * half

    @pl.when(step == 0)
    def start():
        acc[...] = jnp.zeros_like(acc)
        peak_ref[...] = jnp.zeros_like(peak_ref)
        total_ref[...] = jnp.ones_like(total_ref)

    member = lax.broadcasted_iota(jnp.int32, (rows, pairs), 0) == target_ref[0]
    chosen = jnp.where(member, 1.0, 0.0).astype(BF16)
    queries = jnp.dot(latent_t_ref[...], chosen, preferred_element_type=F32)
    scores, fields = [], []
    for parity in range(2):
        part = field_ref[:, parity * half : (parity + 1) * half, :].reshape(pairs, channels)
        keys = lax.dot_general(proj_t_ref[0:width, :], part, NT, preferred_element_type=F32)
        logits = jnp.sum((queries * keys).reshape(heads, size, pairs), axis=1)
        scores.append(logits * (size ** -0.5) + bias_ref[0, parity : parity + 1, :])
        fields.append(part)
    pair_peak = jnp.maximum(scores[0], scores[1])
    lane = lax.broadcasted_iota(jnp.int32, (rows, 128), 1)
    peaks = jnp.full((rows, 128), NEG, F32)
    for head in range(heads):
        column = jnp.max(
            jnp.where(member, pair_peak[head : head + 1, :], NEG), axis=1, keepdims=True
        )
        peaks = jnp.where(lane == head, column, peaks)
    block_peak = peaks.T[0:heads, :]
    old = peak_ref[...]
    new = jnp.maximum(old, block_peak)
    upper = new.astype(BF16)
    lower = (new - upper.astype(F32)).astype(BF16)
    new = upper.astype(F32) + lower.astype(F32)
    peak_ref[...] = new
    factor = jnp.exp(old - new)
    slot_peak = jnp.dot(upper, chosen, preferred_element_type=F32) + jnp.dot(
        lower, chosen, preferred_element_type=F32
    )
    weights = [jnp.exp(score - slot_peak) for score in scores]
    both = weights[0] + weights[1]
    both_upper = both.astype(BF16)
    both_lower = (both - both_upper.astype(F32)).astype(BF16)
    sums = lax.dot_general(both_upper, chosen, NT, preferred_element_type=F32)
    sums = sums + lax.dot_general(both_lower, chosen, NT, preferred_element_type=F32)
    total_ref[...] = total_ref[...] * factor + sums
    mixed = None
    for parity in range(2):
        values = lax.dot_general(
            proj_t_ref[width : 2 * width, :], fields[parity], NT, preferred_element_type=F32
        )
        term = values.reshape(heads, size, pairs) * weights[parity][:, None, :]
        mixed = term if mixed is None else mixed + term
    mixed = mixed.reshape(width, pairs).astype(BF16)
    added = lax.dot_general(mixed, chosen, NT, preferred_element_type=F32)
    acc[...] = (
        acc[...].reshape(heads, size, rows) * factor[:, None, :]
    ).reshape(width, rows) + added

    @pl.when(step == pl.num_programs(0) - 1)
    def finish():
        scale = 1.0 / total_ref[...]
        encoded = (acc[...].reshape(heads, size, rows) * scale[:, None, :]).reshape(width, rows)
        hidden = latent_ref[...].astype(F32) + encoded.T
        hidden_ref[...] = hidden
        center = hidden - jnp.mean(hidden, axis=1, keepdims=True)
        variance = jnp.mean(center * center, axis=1, keepdims=True)
        norm_ref[...] = (center * lax.rsqrt(variance + 1e-05) * gain_ref[...]).astype(BF16)


def attention_kernel(
    last, before_ref, norm_ref, after_ref, hidden_ref, proj_ref, table_ref, out_proj_ref,
    cotangent_ref, processed_ref, grad_ref, extended, pairs, queries, attended,
):
    device = lax.axis_index("seq")
    rows, width = norm_ref.shape
    heads = table_ref.shape[0]
    size = width // heads
    reach = before_ref.shape[0]
    span = 3 * reach
    extended[0:reach, :] = before_ref[...]
    extended[reach : reach + rows, :] = norm_ref[...]
    extended[reach + rows :, :] = after_ref[...]
    tile = 512

    def query_tile(index, carry):
        at = pl.ds(pl.multiple_of(index * tile, tile), tile)
        queries[:, at] = jnp.dot(
            norm_ref[...], proj_ref[:, at], preferred_element_type=F32
        ).astype(BF16)
        return carry

    lax.fori_loop(0, width // tile, query_tile, 0)

    def pair_tile(index, carry):
        at = pl.ds(pl.multiple_of(index * tile, tile), tile)
        here = pl.ds(pl.multiple_of(index * tile + width, tile), tile)
        pairs[:, at] = jnp.dot(
            extended[...], proj_ref[:, here], preferred_element_type=F32
        ).astype(BF16)
        return carry

    lax.fori_loop(0, 2 * width // tile, pair_tile, 0)
    key = lax.broadcasted_iota(jnp.int32, (1, span), 1)
    edges = [
        jnp.where((key < reach) & (device == 0), NEG, 0.0),
        jnp.where((key >= 2 * reach) & (device == last), NEG, 0.0),
    ]
    for head in range(heads):
        columns = slice(head * size, (head + 1) * size)
        value_columns = slice(width + head * size, width + (head + 1) * size)
        row = jnp.broadcast_to(table_ref[head : head + 1, :], (reach, span))
        table = pltpu.roll(row, 0, 1, stride=1, stride_axis=0)
        for block in range(2):
            mine = slice(block * reach, (block + 1) * reach)
            theirs = slice(block * reach, block * reach + span)
            logits = lax.dot_general(
                queries[mine, columns], pairs[theirs, columns], NT, preferred_element_type=F32
            )
            logits = logits * (size ** -0.5) + table + edges[block]
            powered = jnp.exp(logits - jnp.max(logits, axis=1, keepdims=True))
            total = jnp.sum(powered, axis=1, keepdims=True)
            probs = (powered / total).astype(BF16)
            mixture = jnp.dot(probs, pairs[theirs, value_columns], preferred_element_type=F32)
            attended[mine, columns] = mixture.astype(BF16)

    def out_tile(index, carry):
        at = pl.ds(pl.multiple_of(index * tile, tile), tile)
        processed_ref[:, at] = (
            hidden_ref[:, at]
            + jnp.dot(attended[...], out_proj_ref[:, at], preferred_element_type=F32)
        ).astype(BF16)
        return carry

    lax.fori_loop(0, width // tile, out_tile, 0)

    for group in range(X):
        part = lax.dot_general(
            attended[:, group * 256 : (group + 1) * 256], cotangent_ref[0], TN,
            preferred_element_type=F32,
        )
        grad_ref[group * 16 : (group + 1) * 16] = part.astype(BF16).reshape(16, 16, width)


def reduce_kernel(
    grad_ref, out_ref, from_core, merged, x_in, x_sum, z_in, y_all,
    v_in, v_sum, u_in, u_sum, w_in, r_all, send, recv,
):
    seq = lax.axis_index("seq")
    y = lax.axis_index("dp")
    core = seq % CORES
    z = (seq // CORES) % Z
    x = seq // (CORES * Z)

    def at(y_to, x_to, z_to, core_to):
        return (y_to, x_to * (Z * CORES) + z_to * CORES + core_to)

    sibling = at(y, x, z, 1 - core)
    x_peers = [at(y, (x + k) % X, z, core) for k in range(1, X)]
    y_peers = [at((y + k) % Y, x, z, core) for k in range(1, Y)]
    z_peers = [at(y, x, (z + k) % Z, core) for k in range(1, Z)]
    barrier = pltpu.get_barrier_semaphore()
    peers = [sibling] + x_peers + y_peers + z_peers
    for peer in peers:
        pl.semaphore_signal(barrier, inc=1, device_id=peer, device_id_type=MESH)
    pl.semaphore_wait(barrier, len(peers))

    count = iter(range(64))

    def copy(src, dst, peer):
        n = next(count)
        made = pltpu.make_async_remote_copy(
            src_ref=src, dst_ref=dst, send_sem=send.at[n], recv_sem=recv.at[n],
            device_id=peer, device_id_type=MESH,
        )
        made.start()
        return made

    half, quarter = 512, 128
    sent = []
    first = copy(
        grad_ref.at[:, 1 - core, :, 0:half], from_core.at[:, :, 0:half], sibling
    )
    second = copy(
        grad_ref.at[:, 1 - core, :, half:], from_core.at[:, :, half:], sibling
    )
    first.wait_recv()
    merged[:, :, 0:half] = (
        grad_ref[:, core, :, 0:half].astype(F32) + from_core[:, :, 0:half].astype(F32)
    ).astype(BF16)
    x_copies = [
        copy(merged.at[pl.ds(((x + k) % X) * Z, Z), :, 0:half], x_in.at[k - 1], x_peers[k - 1])
        for k in range(1, X)
    ]
    second.wait_recv()
    merged[:, :, half:] = (
        grad_ref[:, core, :, half:].astype(F32) + from_core[:, :, half:].astype(F32)
    ).astype(BF16)

    def strip(who):
        return pl.ds(pl.multiple_of(half + who * quarter, quarter), quarter)

    y_copies = [
        copy(merged.at[:, :, strip((y + k) % Y)], v_in.at[k - 1], y_peers[k - 1])
        for k in range(1, Y)
    ]

    for c in x_copies:
        c.wait_recv()
    x_sum[...] = (
        merged[pl.ds(x * Z, Z), :, 0:half].astype(F32)
        + (x_in[0].astype(F32) + x_in[1].astype(F32) + x_in[2].astype(F32))
    ).astype(BF16)
    z_copies = [
        copy(x_sum.at[(z + k) % Z], z_in.at[k - 1], z_peers[k - 1]) for k in range(1, Z)
    ]
    for c in y_copies:
        c.wait_recv()
    v_sum[...] = (
        merged[:, :, strip(y)].astype(F32)
        + (v_in[0].astype(F32) + v_in[1].astype(F32) + v_in[2].astype(F32))
    ).astype(BF16)
    u_copies = [
        copy(v_sum.at[pl.ds(((x + k) % X) * Z, Z)], u_in.at[k - 1], x_peers[k - 1])
        for k in range(1, X)
    ]
    for c in z_copies:
        c.wait_recv()
    part = x_sum[z].astype(F32)
    for k in range(Z - 1):
        part = part + z_in[k].astype(F32)
    y_all[y] = part
    s_copies = [copy(y_all.at[y], y_all.at[y], y_peers[k - 1]) for k in range(1, Y)]
    for c in u_copies:
        c.wait_recv()
    u_sum[...] = (
        v_sum[pl.ds(x * Z, Z)].astype(F32)
        + (u_in[0].astype(F32) + u_in[1].astype(F32) + u_in[2].astype(F32))
    ).astype(BF16)
    w_copies = [
        copy(u_sum.at[(z + k) % Z], w_in.at[k - 1], z_peers[k - 1]) for k in range(1, Z)
    ]
    for c in w_copies:
        c.wait_recv()
    part = u_sum[z].astype(F32)
    for k in range(Z - 1):
        part = part + w_in[k].astype(F32)
    r_all[y] = part
    r_copies = [copy(r_all.at[y], r_all.at[y], y_peers[k - 1]) for k in range(1, Y)]
    for c in s_copies:
        c.wait_recv()
    out_ref[:, 0:half] = (y_all[0] + y_all[1]) + (y_all[2] + y_all[3])
    for c in r_copies:
        c.wait_recv()
    for k in range(Y):
        out_ref[:, half + k * quarter : half + (k + 1) * quarter] = r_all[k]
    for c in [first, second] + x_copies + y_copies + z_copies + u_copies + s_copies + w_copies + r_copies:
        c.wait_send()


def shards(
    grid_fields, mesh_latent, edge_source, edge_target, edge_count, edge_bias, encoder_proj,
    norm_gain, processor_proj, offset_bias, windows, output_proj, cotangent,
):
    shard_count = lax.axis_size("seq")
    device = lax.axis_index("seq")
    rows, width = mesh_latent.shape
    heads = offset_bias.shape[0]
    reach = (offset_bias.shape[1] - 1) // 2
    channels, points = grid_fields.shape[1:]
    capacity = edge_source.shape[2]

    outgoing = pl.pallas_call(
        gather_kernel,
        out_shape=jax.ShapeDtypeStruct((shard_count, capacity, 128), BF16),
        in_specs=[pl.BlockSpec(memory_space=pltpu.SMEM), vmem()],
        out_specs=vmem(),
        scratch_shapes=[pltpu.VMEM((points, 128), F32), pltpu.VMEM((capacity, 128), F32)],
        compiler_params=pltpu.CompilerParams(vmem_limit_bytes=VMEM_LIMIT),
        name="take_fields",
    )(edge_source[0], grid_fields)
    incoming = lax.all_to_all(outgoing, "seq", split_axis=0, concat_axis=0, tiled=True)

    group = 8
    steps = shard_count // group
    pairs = group * capacity // 2
    own_counts = lax.dynamic_index_in_dim(edge_count, device, 1, keepdims=False)
    live = jnp.arange(capacity, dtype=jnp.int32)[None, :] < own_counts[:, None]
    bias = jnp.where(live, edge_bias[0], NEG)
    bias = bias.reshape(steps, pairs, 2).transpose(0, 2, 1)
    targets = edge_target[0].reshape(steps, pairs, 2)[:, :, 0].reshape(steps, 1, pairs)
    latent_t = mesh_latent.T
    proj_t = jnp.pad(encoder_proj, ((0, 128 - channels), (0, 0))).T
    offset = jnp.arange(3 * reach, dtype=jnp.int32) - reach
    table = jnp.where(
        jnp.abs(offset)[None, :] <= windows[:, None],
        jnp.pad(offset_bias, ((0, 0), (0, reach - 1))),
        NEG,
    )

    whole = lambda *shape: pl.BlockSpec(shape, lambda i: (0,) * len(shape))
    hidden, normalized = pl.pallas_call(
        edge_kernel,
        grid=(steps,),
        out_shape=(
            jax.ShapeDtypeStruct((rows, width), F32),
            jax.ShapeDtypeStruct((rows, width), BF16),
        ),
        in_specs=[
            pl.BlockSpec((group, capacity, 128), lambda i: (i, 0, 0)),
            pl.BlockSpec((1, 1, pairs), lambda i: (i, 0, 0)),
            pl.BlockSpec((1, 2, pairs), lambda i: (i, 0, 0)),
            whole(width, rows),
            whole(2 * width, 128),
            whole(rows, width),
            whole(1, width),
        ],
        out_specs=(whole(rows, width), whole(rows, width)),
        scratch_shapes=[
            pltpu.VMEM((width, rows), F32),
            pltpu.VMEM((heads, rows), F32),
            pltpu.VMEM((heads, rows), F32),
        ],
        compiler_params=pltpu.CompilerParams(vmem_limit_bytes=VMEM_LIMIT),
        name="attend_edges",
    )(incoming, targets, bias, latent_t, proj_t, mesh_latent, norm_gain[None])

    up = [(i, i + 1) for i in range(shard_count - 1)]
    down = [(j, i) for i, j in up]
    before = lax.ppermute(normalized[rows - reach :], "seq", up)
    after = lax.ppermute(normalized[:reach], "seq", down)

    processed, grad = pl.pallas_call(
        functools.partial(attention_kernel, shard_count - 1),
        out_shape=(
            jax.ShapeDtypeStruct((rows, width), BF16),
            jax.ShapeDtypeStruct((width // 16, 16, width), BF16),
        ),
        in_specs=[vmem()] * 8,
        out_specs=(vmem(), vmem()),
        scratch_shapes=[
            pltpu.VMEM((rows + 2 * reach, width), BF16),
            pltpu.VMEM((rows + 2 * reach, 2 * width), BF16),
            pltpu.VMEM((rows, width), BF16),
            pltpu.VMEM((rows, width), BF16),
        ],
        compiler_params=pltpu.CompilerParams(vmem_limit_bytes=VMEM_LIMIT),
        name="window_attention",
    )(before, normalized, after, hidden, processor_proj, table, output_proj, cotangent)

    gradient = pl.pallas_call(
        reduce_kernel,
        out_shape=jax.ShapeDtypeStruct((16, width), F32),
        in_specs=[vmem()],
        out_specs=vmem(),
        scratch_shapes=[
            pltpu.VMEM((32, 16, 1024), BF16),
            pltpu.VMEM((32, 16, 1024), BF16),
            pltpu.VMEM((3, 8, 16, 512), BF16),
            pltpu.VMEM((8, 16, 512), BF16),
            pltpu.VMEM((7, 16, 512), BF16),
            pltpu.VMEM((4, 16, 512), F32),
            pltpu.VMEM((3, 32, 16, 128), BF16),
            pltpu.VMEM((32, 16, 128), BF16),
            pltpu.VMEM((3, 8, 16, 128), BF16),
            pltpu.VMEM((8, 16, 128), BF16),
            pltpu.VMEM((7, 16, 128), BF16),
            pltpu.VMEM((4, 16, 128), F32),
            pltpu.SemaphoreType.DMA((64,)),
            pltpu.SemaphoreType.DMA((64,)),
        ],
        compiler_params=pltpu.CompilerParams(
            vmem_limit_bytes=VMEM_LIMIT, collective_id=1, has_side_effects=True
        ),
        name="reduce_gradient",
    )(grad.reshape(32, 2, 16, width))
    return (processed[None], gradient)


def solution(mesh):
    in_specs = (
        P("dp", None, "seq"),
        P("seq", None),
        P("seq", None, None),
        P("seq", None, None),
        P(),
        P("seq", None, None),
        P(),
        P(),
        P(),
        P(),
        P(),
        P(),
        P("dp", "seq", None),
    )
    out_specs = (P("dp", "seq", None), P("seq", None))
    return jax.shard_map(shards, mesh=mesh, in_specs=in_specs, out_specs=out_specs, check_vma=False)
```

```python
import functools

import jax
import jax.numpy as jnp
from jax import lax
from jax.experimental import pallas as pl
from jax.experimental.pallas import tpu as pltpu
from jax.sharding import PartitionSpec as P

MESH = pl.DeviceIdType.MESH
X, Z, CORES, Y = 4, 8, 2, 4
NEG = -1e30
F32 = jnp.float32
BF16 = jnp.bfloat16
VMEM_LIMIT = 56 * 1024 * 1024

NT = (((1,), (1,)), ((), ()))
TN = (((0,), (0,)), ((), ()))


def vmem():
    return pl.BlockSpec(memory_space=pltpu.VMEM)


def encode_kernel(
    source_ref, grid_ref, target_ref, count_ref, bias_ref, latent_ref, proj_ref, gain_ref,
    hidden_ref, norm_ref, table, stage, outgoing, incoming, latent_t, proj_t, counts,
    targets, biases, acc, peak_ref, total_ref, send, recv,
):
    seq = lax.axis_index("seq")
    y = lax.axis_index("dp")
    core = seq % CORES
    z = (seq // CORES) % Z
    x = seq // (CORES * Z)
    channels = grid_ref.shape[1]
    owners, capacity = source_ref.shape
    rows, width = latent_ref.shape
    heads = peak_ref.shape[0]
    size = width // heads
    half = capacity // 2
    group = 2 * X
    depth = outgoing.shape[1]

    def z_shift(turn):
        return 4 + (1 - 2 * (turn % 2)) * ((turn + 1) // 2)

    barrier = pltpu.get_barrier_semaphore()

    def greet(offset, carry):
        pl.semaphore_signal(
            barrier, inc=1, device_id=(y, (seq + offset) % owners), device_id_type=MESH
        )
        return carry

    lax.fori_loop(1, owners, greet, 0)
    stage[...] = jnp.zeros_like(stage)

    def turn_fields(chunk, carry):
        start = pl.multiple_of(chunk * 128, 128)
        stage[0:channels, :] = grid_ref[0, :, pl.ds(start, 128)].astype(F32)
        table[pl.ds(start, 128), :] = stage[...].T
        return carry

    lax.fori_loop(0, grid_ref.shape[2] // 128, turn_fields, 0)
    pl.semaphore_wait(barrier, owners - 1)

    def block_copy(step):
        to_x = (x + (step // CORES) % X) % X
        to_z = (z + z_shift(step // group)) % Z
        to = to_x * (Z * CORES) + to_z * CORES + step % CORES
        slot = step - step % CORES + core
        copy = pltpu.make_async_remote_copy(
            src_ref=outgoing.at[step], dst_ref=incoming.at[slot],
            send_sem=send.at[step], recv_sem=recv.at[slot],
            device_id=(y, to), device_id_type=MESH,
        )
        return to, copy

    def send_step(step, carry):
        to, copy = block_copy(step)
        for slot in range(capacity):
            row = (slot % 2) * half + slot // 2
            stage[row : row + 1, :] = table[pl.ds(source_ref[to, slot], 1), :]
        block = stage[...].T[0:depth, :].astype(BF16)

        @pl.when(to == seq)
        def keep():
            incoming[step] = block

        @pl.when(to != seq)
        def pass_on():
            outgoing[step] = block
            copy.start()

        return carry

    lax.fori_loop(0, owners, send_step, 0)

    for chunk in range(width // 128):
        here = slice(chunk * 128, (chunk + 1) * 128)
        latent_t[here, :] = latent_ref[:, here].astype(F32).T.astype(BF16)
    stage[...] = jnp.zeros_like(stage)

    def turn_proj(chunk, carry):
        start = pl.multiple_of(chunk * 128, 128)
        stage[0:channels, :] = proj_ref[:, pl.ds(start, 128)].astype(F32)
        proj_t[pl.ds(start, 128), :] = stage[...].T.astype(BF16)
        return carry

    lax.fori_loop(0, 2 * width // 128, turn_proj, 0)

    chips = owners // CORES
    lane = lax.broadcasted_iota(jnp.int32, (chips, capacity), 1)
    slot_row = lax.broadcasted_iota(jnp.int32, (capacity, capacity), 0)
    slot_lane = lax.broadcasted_iota(jnp.int32, (capacity, capacity), 1)
    owner_lane = lax.broadcasted_iota(jnp.int32, (owners, owners), 1)
    own = jnp.sum(jnp.where(owner_lane == seq, count_ref[...], 0), axis=1, keepdims=True)
    counts[...] = jnp.broadcast_to(own, (owners, capacity))

    def of_core(ref, which):
        return ref[pl.ds(which, chips, stride=CORES), :]

    def picks(parity, which):
        wanted = slot_row == 2 * (slot_lane - which * half) + parity
        in_half = (slot_lane >= which * half) & (slot_lane < (which + 1) * half)
        return jnp.where(wanted & in_half, 1.0, 0.0)

    found = jnp.zeros((chips, capacity), F32)
    for which in range(CORES):
        found = found + jnp.dot(
            of_core(target_ref, which).astype(F32), picks(0, which),
            precision=lax.Precision.HIGHEST, preferred_element_type=F32,
        )
    targets[...] = found.astype(jnp.int32)
    live = jnp.where(lane < half, of_core(counts, 0), of_core(counts, 1))
    for parity in range(2):
        found = jnp.zeros((chips, capacity), F32)
        for which in range(CORES):
            found = found + jnp.dot(
                of_core(bias_ref, which), picks(parity, which),
                precision=lax.Precision.HIGHEST, preferred_element_type=F32,
            )
        biases[parity] = jnp.where(2 * (lane % half) + parity < live, found, NEG)

    acc[...] = jnp.zeros_like(acc)
    peak_ref[...] = jnp.zeros_like(peak_ref)
    total_ref[...] = jnp.ones_like(total_ref)
    pairs = X * capacity
    low = lax.broadcasted_iota(jnp.int32, (depth, capacity), 1) < half
    peak_lane = lax.broadcasted_iota(jnp.int32, (rows, 128), 1)
    row_index = lax.broadcasted_iota(jnp.int32, (rows, pairs), 0)

    def group_step(turn, carry):
        for member_at in range(group):
            slot = turn * group + member_at

            @pl.when(slot != (Z - 1) * group + core)
            def arrive():
                pltpu.make_async_copy(
                    incoming.at[slot], incoming.at[slot], recv.at[slot]
                ).wait()

        evens, odds, rows_of, bias_of = [], [], [], [[], []]
        for shift in range(X):
            first = incoming[turn * group + CORES * shift].astype(F32)
            second = incoming[turn * group + CORES * shift + 1].astype(F32)
            evens.append(jnp.where(low, first, pltpu.roll(second, half, 1)).astype(BF16))
            odds.append(jnp.where(low, pltpu.roll(first, half, 1), second).astype(BF16))
            chip = ((x + X - shift) % X) * Z + (z + Z - z_shift(turn)) % Z
            rows_of.append(targets[pl.ds(chip, 1), :])
            for parity in range(2):
                bias_of[parity].append(biases[parity, pl.ds(chip, 1), :])
        target = jnp.concatenate(rows_of, axis=1)
        member = row_index == target
        chosen = jnp.where(member, 1.0, 0.0).astype(BF16)
        queries = jnp.dot(latent_t[...], chosen, preferred_element_type=F32)
        scores, fields = [], []
        for parity, parts in enumerate((evens, odds)):
            part = jnp.concatenate(parts, axis=1)
            keys = jnp.dot(proj_t[0:width, 0:depth], part, preferred_element_type=F32)
            logits = jnp.sum((queries * keys).reshape(heads, size, pairs), axis=1)
            scores.append(logits * (size ** -0.5) + jnp.concatenate(bias_of[parity], axis=1))
            fields.append(part)
        pair_peak = jnp.maximum(scores[0], scores[1])
        peaks = jnp.full((rows, 128), NEG, F32)
        for head in range(heads):
            column = jnp.max(
                jnp.where(member, pair_peak[head : head + 1, :], NEG), axis=1, keepdims=True
            )
            peaks = jnp.where(peak_lane == head, column, peaks)
        old = peak_ref[...]
        new = jnp.maximum(old, peaks.T[0:heads, :])
        upper = new.astype(BF16)
        lower = (new - upper.astype(F32)).astype(BF16)
        new = upper.astype(F32) + lower.astype(F32)
        peak_ref[...] = new
        factor = jnp.exp(old - new)
        slot_peak = jnp.dot(upper, chosen, preferred_element_type=F32) + jnp.dot(
            lower, chosen, preferred_element_type=F32
        )
        weights = [jnp.exp(score - slot_peak) for score in scores]
        both = weights[0] + weights[1]
        both_upper = both.astype(BF16)
        both_lower = (both - both_upper.astype(F32)).astype(BF16)
        sums = lax.dot_general(both_upper, chosen, NT, preferred_element_type=F32)
        sums = sums + lax.dot_general(both_lower, chosen, NT, preferred_element_type=F32)
        total_ref[...] = total_ref[...] * factor + sums
        mixed = None
        for parity in range(2):
            values = jnp.dot(
                proj_t[width : 2 * width, 0:depth], fields[parity], preferred_element_type=F32
            )
            term = values.reshape(heads, size, pairs) * weights[parity][:, None, :]
            mixed = term if mixed is None else mixed + term
        mixed = mixed.reshape(width, pairs).astype(BF16)
        added = lax.dot_general(mixed, chosen, NT, preferred_element_type=F32)
        acc[...] = (
            acc[...].reshape(heads, size, rows) * factor[:, None, :]
        ).reshape(width, rows) + added
        return carry

    lax.fori_loop(0, Z, group_step, 0)

    scale = 1.0 / total_ref[...]
    encoded = (acc[...].reshape(heads, size, rows) * scale[:, None, :]).reshape(width, rows)
    hidden = latent_ref[...].astype(F32) + encoded.T
    hidden_ref[...] = hidden
    center = hidden - jnp.mean(hidden, axis=1, keepdims=True)
    variance = jnp.mean(center * center, axis=1, keepdims=True)
    norm_ref[...] = (center * lax.rsqrt(variance + 1e-05) * gain_ref[...]).astype(BF16)

    def sent_step(step, carry):
        to, copy = block_copy(step)

        @pl.when(to != seq)
        def done():
            copy.wait_send()

        return carry

    lax.fori_loop(0, owners, sent_step, 0)


def attention_kernel(
    last, before_ref, norm_ref, after_ref, hidden_ref, proj_ref, table_ref, out_proj_ref,
    cotangent_ref, processed_ref, grad_ref, extended, pairs, queries, attended,
):
    device = lax.axis_index("seq")
    rows, width = norm_ref.shape
    heads = table_ref.shape[0]
    size = width // heads
    reach = before_ref.shape[0]
    span = 3 * reach
    extended[0:reach, :] = before_ref[...]
    extended[reach : reach + rows, :] = norm_ref[...]
    extended[reach + rows :, :] = after_ref[...]
    tile = 512

    def query_tile(index, carry):
        at = pl.ds(pl.multiple_of(index * tile, tile), tile)
        queries[:, at] = jnp.dot(
            norm_ref[...], proj_ref[:, at], preferred_element_type=F32
        ).astype(BF16)
        return carry

    lax.fori_loop(0, width // tile, query_tile, 0)

    def pair_tile(index, carry):
        at = pl.ds(pl.multiple_of(index * tile, tile), tile)
        here = pl.ds(pl.multiple_of(index * tile + width, tile), tile)
        pairs[:, at] = jnp.dot(
            extended[...], proj_ref[:, here], preferred_element_type=F32
        ).astype(BF16)
        return carry

    lax.fori_loop(0, 2 * width // tile, pair_tile, 0)
    key = lax.broadcasted_iota(jnp.int32, (1, span), 1)
    edges = [
        jnp.where((key < reach) & (device == 0), NEG, 0.0),
        jnp.where((key >= 2 * reach) & (device == last), NEG, 0.0),
    ]
    for head in range(heads):
        columns = slice(head * size, (head + 1) * size)
        value_columns = slice(width + head * size, width + (head + 1) * size)
        row = jnp.broadcast_to(table_ref[head : head + 1, :], (reach, span))
        table = pltpu.roll(row, 0, 1, stride=1, stride_axis=0)
        for block in range(2):
            mine = slice(block * reach, (block + 1) * reach)
            theirs = slice(block * reach, block * reach + span)
            logits = lax.dot_general(
                queries[mine, columns], pairs[theirs, columns], NT, preferred_element_type=F32
            )
            logits = logits * (size ** -0.5) + table + edges[block]
            powered = jnp.exp(logits - jnp.max(logits, axis=1, keepdims=True))
            total = jnp.sum(powered, axis=1, keepdims=True)
            probs = (powered / total).astype(BF16)
            mixture = jnp.dot(probs, pairs[theirs, value_columns], preferred_element_type=F32)
            attended[mine, columns] = mixture.astype(BF16)

    def out_tile(index, carry):
        at = pl.ds(pl.multiple_of(index * tile, tile), tile)
        processed_ref[:, at] = (
            hidden_ref[:, at]
            + jnp.dot(attended[...], out_proj_ref[:, at], preferred_element_type=F32)
        ).astype(BF16)
        return carry

    lax.fori_loop(0, width // tile, out_tile, 0)

    for group in range(X):
        part = lax.dot_general(
            attended[:, group * 256 : (group + 1) * 256], cotangent_ref[0], TN,
            preferred_element_type=F32,
        )
        grad_ref[group * 16 : (group + 1) * 16] = part.astype(BF16).reshape(16, 16, width)


def reduce_kernel(
    grad_ref, out_ref, from_core, merged, x_in, x_sum, z_in, y_all,
    v_in, v_sum, u_in, u_sum, w_in, r_all, send, recv,
):
    seq = lax.axis_index("seq")
    y = lax.axis_index("dp")
    core = seq % CORES
    z = (seq // CORES) % Z
    x = seq // (CORES * Z)

    def at(y_to, x_to, z_to, core_to):
        return (y_to, x_to * (Z * CORES) + z_to * CORES + core_to)

    sibling = at(y, x, z, 1 - core)
    x_peers = [at(y, (x + k) % X, z, core) for k in range(1, X)]
    y_peers = [at((y + k) % Y, x, z, core) for k in range(1, Y)]
    z_peers = [at(y, x, (z + k) % Z, core) for k in range(1, Z)]
    barrier = pltpu.get_barrier_semaphore()
    peers = [sibling] + x_peers + y_peers + z_peers
    for peer in peers:
        pl.semaphore_signal(barrier, inc=1, device_id=peer, device_id_type=MESH)
    pl.semaphore_wait(barrier, len(peers))

    count = iter(range(64))

    def copy(src, dst, peer):
        n = next(count)
        made = pltpu.make_async_remote_copy(
            src_ref=src, dst_ref=dst, send_sem=send.at[n], recv_sem=recv.at[n],
            device_id=peer, device_id_type=MESH,
        )
        made.start()
        return made

    half, quarter = 512, 128
    sent = []
    first = copy(
        grad_ref.at[:, 1 - core, :, 0:half], from_core.at[:, :, 0:half], sibling
    )
    second = copy(
        grad_ref.at[:, 1 - core, :, half:], from_core.at[:, :, half:], sibling
    )
    first.wait_recv()
    merged[:, :, 0:half] = (
        grad_ref[:, core, :, 0:half].astype(F32) + from_core[:, :, 0:half].astype(F32)
    ).astype(BF16)
    x_copies = [
        copy(merged.at[pl.ds(((x + k) % X) * Z, Z), :, 0:half], x_in.at[k - 1], x_peers[k - 1])
        for k in range(1, X)
    ]
    second.wait_recv()
    merged[:, :, half:] = (
        grad_ref[:, core, :, half:].astype(F32) + from_core[:, :, half:].astype(F32)
    ).astype(BF16)

    def strip(who):
        return pl.ds(pl.multiple_of(half + who * quarter, quarter), quarter)

    y_copies = [
        copy(merged.at[:, :, strip((y + k) % Y)], v_in.at[k - 1], y_peers[k - 1])
        for k in range(1, Y)
    ]

    for c in x_copies:
        c.wait_recv()
    x_sum[...] = (
        merged[pl.ds(x * Z, Z), :, 0:half].astype(F32)
        + (x_in[0].astype(F32) + x_in[1].astype(F32) + x_in[2].astype(F32))
    ).astype(BF16)
    z_copies = [
        copy(x_sum.at[(z + k) % Z], z_in.at[k - 1], z_peers[k - 1]) for k in range(1, Z)
    ]
    for c in y_copies:
        c.wait_recv()
    v_sum[...] = (
        merged[:, :, strip(y)].astype(F32)
        + (v_in[0].astype(F32) + v_in[1].astype(F32) + v_in[2].astype(F32))
    ).astype(BF16)
    u_copies = [
        copy(v_sum.at[pl.ds(((x + k) % X) * Z, Z)], u_in.at[k - 1], x_peers[k - 1])
        for k in range(1, X)
    ]
    for c in z_copies:
        c.wait_recv()
    part = x_sum[z].astype(F32)
    for k in range(Z - 1):
        part = part + z_in[k].astype(F32)
    y_all[y] = part
    s_copies = [copy(y_all.at[y], y_all.at[y], y_peers[k - 1]) for k in range(1, Y)]
    for c in u_copies:
        c.wait_recv()
    u_sum[...] = (
        v_sum[pl.ds(x * Z, Z)].astype(F32)
        + (u_in[0].astype(F32) + u_in[1].astype(F32) + u_in[2].astype(F32))
    ).astype(BF16)
    w_copies = [
        copy(u_sum.at[(z + k) % Z], w_in.at[k - 1], z_peers[k - 1]) for k in range(1, Z)
    ]
    for c in w_copies:
        c.wait_recv()
    part = u_sum[z].astype(F32)
    for k in range(Z - 1):
        part = part + w_in[k].astype(F32)
    r_all[y] = part
    r_copies = [copy(r_all.at[y], r_all.at[y], y_peers[k - 1]) for k in range(1, Y)]
    for c in s_copies:
        c.wait_recv()
    out_ref[:, 0:half] = (y_all[0] + y_all[1]) + (y_all[2] + y_all[3])
    for c in r_copies:
        c.wait_recv()
    for k in range(Y):
        out_ref[:, half + k * quarter : half + (k + 1) * quarter] = r_all[k]
    for c in [first, second] + x_copies + y_copies + z_copies + u_copies + s_copies + w_copies + r_copies:
        c.wait_send()


def shards(
    grid_fields, mesh_latent, edge_source, edge_target, edge_count, edge_bias, encoder_proj,
    norm_gain, processor_proj, offset_bias, windows, output_proj, cotangent,
):
    shard_count = lax.axis_size("seq")
    device = lax.axis_index("seq")
    rows, width = mesh_latent.shape
    heads = offset_bias.shape[0]
    reach = (offset_bias.shape[1] - 1) // 2
    channels, points = grid_fields.shape[1:]
    capacity = edge_source.shape[2]
    offset = jnp.arange(3 * reach, dtype=jnp.int32) - reach
    table = jnp.where(
        jnp.abs(offset)[None, :] <= windows[:, None],
        jnp.pad(offset_bias, ((0, 0), (0, reach - 1))),
        NEG,
    )
    depth = (channels + 15) // 16 * 16
    hidden, normalized = pl.pallas_call(
        encode_kernel,
        out_shape=(
            jax.ShapeDtypeStruct((rows, width), F32),
            jax.ShapeDtypeStruct((rows, width), BF16),
        ),
        in_specs=[pl.BlockSpec(memory_space=pltpu.SMEM)] + [vmem()] * 7,
        out_specs=(vmem(), vmem()),
        scratch_shapes=[
            pltpu.VMEM((points, 128), F32),
            pltpu.VMEM((128, 128), F32),
            pltpu.VMEM((shard_count, depth, capacity), BF16),
            pltpu.VMEM((shard_count, depth, capacity), BF16),
            pltpu.VMEM((width, rows), BF16),
            pltpu.VMEM((2 * width, 128), BF16),
            pltpu.VMEM((shard_count, capacity), jnp.int32),
            pltpu.VMEM((shard_count // CORES, capacity), jnp.int32),
            pltpu.VMEM((2, shard_count // CORES, capacity), F32),
            pltpu.VMEM((width, rows), F32),
            pltpu.VMEM((heads, rows), F32),
            pltpu.VMEM((heads, rows), F32),
            pltpu.SemaphoreType.DMA((shard_count,)),
            pltpu.SemaphoreType.DMA((shard_count,)),
        ],
        compiler_params=pltpu.CompilerParams(
            vmem_limit_bytes=VMEM_LIMIT, collective_id=2, has_side_effects=True
        ),
        name="encode",
    )(
        edge_source[0], grid_fields, edge_target[0], edge_count, edge_bias[0], mesh_latent,
        encoder_proj, norm_gain[None],
    )

    up = [(i, i + 1) for i in range(shard_count - 1)]
    down = [(j, i) for i, j in up]
    before = lax.ppermute(normalized[rows - reach :], "seq", up)
    after = lax.ppermute(normalized[:reach], "seq", down)

    processed, grad = pl.pallas_call(
        functools.partial(attention_kernel, shard_count - 1),
        out_shape=(
            jax.ShapeDtypeStruct((rows, width), BF16),
            jax.ShapeDtypeStruct((width // 16, 16, width), BF16),
        ),
        in_specs=[vmem()] * 8,
        out_specs=(vmem(), vmem()),
        scratch_shapes=[
            pltpu.VMEM((rows + 2 * reach, width), BF16),
            pltpu.VMEM((rows + 2 * reach, 2 * width), BF16),
            pltpu.VMEM((rows, width), BF16),
            pltpu.VMEM((rows, width), BF16),
        ],
        compiler_params=pltpu.CompilerParams(vmem_limit_bytes=VMEM_LIMIT),
        name="window_attention",
    )(before, normalized, after, hidden, processor_proj, table, output_proj, cotangent)

    gradient = pl.pallas_call(
        reduce_kernel,
        out_shape=jax.ShapeDtypeStruct((16, width), F32),
        in_specs=[vmem()],
        out_specs=vmem(),
        scratch_shapes=[
            pltpu.VMEM((32, 16, 1024), BF16),
            pltpu.VMEM((32, 16, 1024), BF16),
            pltpu.VMEM((3, 8, 16, 512), BF16),
            pltpu.VMEM((8, 16, 512), BF16),
            pltpu.VMEM((7, 16, 512), BF16),
            pltpu.VMEM((4, 16, 512), F32),
            pltpu.VMEM((3, 32, 16, 128), BF16),
            pltpu.VMEM((32, 16, 128), BF16),
            pltpu.VMEM((3, 8, 16, 128), BF16),
            pltpu.VMEM((8, 16, 128), BF16),
            pltpu.VMEM((7, 16, 128), BF16),
            pltpu.VMEM((4, 16, 128), F32),
            pltpu.SemaphoreType.DMA((64,)),
            pltpu.SemaphoreType.DMA((64,)),
        ],
        compiler_params=pltpu.CompilerParams(
            vmem_limit_bytes=VMEM_LIMIT, collective_id=1, has_side_effects=True
        ),
        name="reduce_gradient",
    )(grad.reshape(32, 2, 16, width))
    return (processed[None], gradient)


def solution(mesh):
    in_specs = (
        P("dp", None, "seq"),
        P("seq", None),
        P("seq", None, None),
        P("seq", None, None),
        P(),
        P("seq", None, None),
        P(),
        P(),
        P(),
        P(),
        P(),
        P(),
        P("dp", "seq", None),
    )
    out_specs = (P("dp", "seq", None), P("seq", None))
    return jax.shard_map(shards, mesh=mesh, in_specs=in_specs, out_specs=out_specs, check_vma=False)
```

```python
import jax
import jax.numpy as jnp
from jax import lax
from jax.experimental import pallas as pl
from jax.experimental.pallas import tpu as pltpu
from jax.sharding import PartitionSpec as P

MESH = pl.DeviceIdType.MESH
X, Z, CORES, Y = 4, 8, 2, 4
NEG = -1e30
F32 = jnp.float32
BF16 = jnp.bfloat16
VMEM_LIMIT = 56 * 1024 * 1024

NT = (((1,), (1,)), ((), ()))
TN = (((0,), (0,)), ((), ()))


def vmem():
    return pl.BlockSpec(memory_space=pltpu.VMEM)


def layer_kernel(
    source_ref, grid_ref, target_ref, count_ref, bias_ref, latent_ref, proj_ref, gain_ref,
    offset_ref, big_hbm, out_hbm, cotangent_hbm,
    processed_ref, gradient_ref, table, stage, outgoing, incoming, latent_t, proj_t, counts,
    targets, biases, acc, peak_ref, total_ref, send, recv,
    big, out_proj, cotangent, fetched, hidden_ref, extended, mixed_rows, tables, attended,
    halo_send, halo_recv, grads, from_core, merged, x_in, x_sum, z_in, y_all, v_in, v_sum,
    u_in, u_sum, w_in, r_all, core_send, core_recv, x_send, x_recv, y_send, y_recv, z_send,
    z_recv, s_send, s_recv, u_send, u_recv, w_send, w_recv, r_send, r_recv,
):
    seq = lax.axis_index("seq")
    y = lax.axis_index("dp")
    core = seq % CORES
    z = (seq // CORES) % Z
    x = seq // (CORES * Z)
    channels = grid_ref.shape[1]
    owners, capacity = source_ref.shape
    rows, width = latent_ref.shape
    heads = peak_ref.shape[0]
    size = width // heads
    half = capacity // 2
    group = 2 * X
    depth = outgoing.shape[1]

    def z_shift(turn):
        return 4 + (1 - 2 * (turn % 2)) * ((turn + 1) // 2)

    barrier = pltpu.get_barrier_semaphore()

    def greet(offset, carry):
        pl.semaphore_signal(
            barrier, inc=1, device_id=(y, (seq + offset) % owners), device_id_type=MESH
        )
        return carry

    lax.fori_loop(1, owners, greet, 0)
    y_peers = [((y + k) % Y, seq) for k in range(1, Y)]
    for peer in y_peers:
        pl.semaphore_signal(barrier, inc=1, device_id=peer, device_id_type=MESH)
    fetches = [
        pltpu.make_async_copy(big_hbm, big, fetched.at[0]),
        pltpu.make_async_copy(out_hbm, out_proj, fetched.at[1]),
        pltpu.make_async_copy(cotangent_hbm, cotangent, fetched.at[2]),
    ]
    for fetch in fetches:
        fetch.start()
    stage[...] = jnp.zeros_like(stage)

    def turn_fields(chunk, carry):
        start = pl.multiple_of(chunk * 128, 128)
        stage[0:channels, :] = grid_ref[0, :, pl.ds(start, 128)].astype(F32)
        table[pl.ds(start, 128), :] = stage[...].T
        return carry

    lax.fori_loop(0, grid_ref.shape[2] // 128, turn_fields, 0)
    pl.semaphore_wait(barrier, owners - 1 + Y - 1)

    def block_copy(step):
        to_x = (x + (step // CORES) % X) % X
        to_z = (z + z_shift(step // group)) % Z
        to = to_x * (Z * CORES) + to_z * CORES + step % CORES
        slot = step - step % CORES + core
        copy = pltpu.make_async_remote_copy(
            src_ref=outgoing.at[step], dst_ref=incoming.at[slot],
            send_sem=send.at[step], recv_sem=recv.at[slot],
            device_id=(y, to), device_id_type=MESH,
        )
        return to, copy

    def send_step(step, carry):
        to, copy = block_copy(step)
        for slot in range(capacity):
            row = (slot % 2) * half + slot // 2
            stage[row : row + 1, :] = table[pl.ds(source_ref[to, slot], 1), :]
        block = stage[...].T[0:depth, :].astype(BF16)

        @pl.when(to == seq)
        def keep():
            incoming[step] = block

        @pl.when(to != seq)
        def pass_on():
            outgoing[step] = block
            copy.start()

        return carry

    lax.fori_loop(0, owners, send_step, 0)

    for chunk in range(width // 128):
        here = slice(chunk * 128, (chunk + 1) * 128)
        latent_t[here, :] = latent_ref[:, here].astype(F32).T.astype(BF16)
    stage[...] = jnp.zeros_like(stage)

    def turn_proj(chunk, carry):
        start = pl.multiple_of(chunk * 128, 128)
        stage[0:channels, :] = proj_ref[:, pl.ds(start, 128)].astype(F32)
        proj_t[pl.ds(start, 128), :] = stage[...].T.astype(BF16)
        return carry

    lax.fori_loop(0, 2 * width // 128, turn_proj, 0)

    chips = owners // CORES
    lane = lax.broadcasted_iota(jnp.int32, (chips, capacity), 1)
    slot_row = lax.broadcasted_iota(jnp.int32, (capacity, capacity), 0)
    slot_lane = lax.broadcasted_iota(jnp.int32, (capacity, capacity), 1)
    owner_lane = lax.broadcasted_iota(jnp.int32, (owners, owners), 1)
    own = jnp.sum(jnp.where(owner_lane == seq, count_ref[...], 0), axis=1, keepdims=True)
    counts[...] = jnp.broadcast_to(own, (owners, capacity))

    def of_core(ref, which):
        return ref[pl.ds(which, chips, stride=CORES), :]

    def picks(parity, which):
        wanted = slot_row == 2 * (slot_lane - which * half) + parity
        in_half = (slot_lane >= which * half) & (slot_lane < (which + 1) * half)
        return jnp.where(wanted & in_half, 1.0, 0.0)

    found = jnp.zeros((chips, capacity), F32)
    for which in range(CORES):
        found = found + jnp.dot(
            of_core(target_ref, which).astype(F32), picks(0, which),
            precision=lax.Precision.HIGHEST, preferred_element_type=F32,
        )
    targets[...] = found.astype(jnp.int32)
    live = jnp.where(lane < half, of_core(counts, 0), of_core(counts, 1))
    for parity in range(2):
        found = jnp.zeros((chips, capacity), F32)
        for which in range(CORES):
            found = found + jnp.dot(
                of_core(bias_ref, which), picks(parity, which),
                precision=lax.Precision.HIGHEST, preferred_element_type=F32,
            )
        biases[parity] = jnp.where(2 * (lane % half) + parity < live, found, NEG)

    reach = tables.shape[2]
    span = tables.shape[3]
    last = owners - 1

    @pl.when(seq == 0)
    def no_before():
        extended[0:reach, :] = jnp.zeros((reach, width), BF16)

    @pl.when(seq == last)
    def no_after():
        extended[reach + rows :, :] = jnp.zeros((reach, width), BF16)

    key_at = lax.broadcasted_iota(jnp.int32, (1, span), 1)
    edges = [
        jnp.where((key_at < reach) & (seq == 0), NEG, 0.0),
        jnp.where((key_at >= 2 * reach) & (seq == last), NEG, 0.0),
    ]

    def table_step(head, carry):
        row = jnp.broadcast_to(offset_ref[pl.ds(head, 1), :], (reach, span))
        spread = pltpu.roll(row, 0, 1, stride=1, stride_axis=0)
        for block in range(2):
            tables[block, head] = spread + edges[block]
        return carry

    lax.fori_loop(0, heads, table_step, 0)

    acc[...] = jnp.zeros_like(acc)
    peak_ref[...] = jnp.zeros_like(peak_ref)
    total_ref[...] = jnp.ones_like(total_ref)
    pairs = X * capacity
    low = lax.broadcasted_iota(jnp.int32, (depth, capacity), 1) < half
    peak_lane = lax.broadcasted_iota(jnp.int32, (rows, 128), 1)
    row_index = lax.broadcasted_iota(jnp.int32, (rows, pairs), 0)

    def group_step(turn, carry):
        for member_at in range(group):
            slot = turn * group + member_at

            @pl.when(slot != (Z - 1) * group + core)
            def arrive():
                pltpu.make_async_copy(
                    incoming.at[slot], incoming.at[slot], recv.at[slot]
                ).wait()

        evens, odds, rows_of, bias_of = [], [], [], [[], []]
        for shift in range(X):
            first = incoming[turn * group + CORES * shift].astype(F32)
            second = incoming[turn * group + CORES * shift + 1].astype(F32)
            evens.append(jnp.where(low, first, pltpu.roll(second, half, 1)).astype(BF16))
            odds.append(jnp.where(low, pltpu.roll(first, half, 1), second).astype(BF16))
            chip = ((x + X - shift) % X) * Z + (z + Z - z_shift(turn)) % Z
            rows_of.append(targets[pl.ds(chip, 1), :])
            for parity in range(2):
                bias_of[parity].append(biases[parity, pl.ds(chip, 1), :])
        target = jnp.concatenate(rows_of, axis=1)
        member = row_index == target
        chosen = jnp.where(member, 1.0, 0.0).astype(BF16)
        queries = jnp.dot(latent_t[...], chosen, preferred_element_type=F32)
        scores, fields = [], []
        for parity, parts in enumerate((evens, odds)):
            part = jnp.concatenate(parts, axis=1)
            keys = jnp.dot(proj_t[0:width, 0:depth], part, preferred_element_type=F32)
            logits = jnp.sum((queries * keys).reshape(heads, size, pairs), axis=1)
            scores.append(logits * (size ** -0.5) + jnp.concatenate(bias_of[parity], axis=1))
            fields.append(part)
        pair_peak = jnp.maximum(scores[0], scores[1])
        peaks = jnp.full((rows, 128), NEG, F32)
        for head in range(heads):
            column = jnp.max(
                jnp.where(member, pair_peak[head : head + 1, :], NEG), axis=1, keepdims=True
            )
            peaks = jnp.where(peak_lane == head, column, peaks)
        old = peak_ref[...]
        new = jnp.maximum(old, peaks.T[0:heads, :])
        upper = new.astype(BF16)
        lower = (new - upper.astype(F32)).astype(BF16)
        new = upper.astype(F32) + lower.astype(F32)
        peak_ref[...] = new
        factor = jnp.exp(old - new)
        slot_peak = jnp.dot(upper, chosen, preferred_element_type=F32) + jnp.dot(
            lower, chosen, preferred_element_type=F32
        )
        weights = [jnp.exp(score - slot_peak) for score in scores]
        both = weights[0] + weights[1]
        both_upper = both.astype(BF16)
        both_lower = (both - both_upper.astype(F32)).astype(BF16)
        sums = lax.dot_general(both_upper, chosen, NT, preferred_element_type=F32)
        sums = sums + lax.dot_general(both_lower, chosen, NT, preferred_element_type=F32)
        total_ref[...] = total_ref[...] * factor + sums
        mixed = None
        for parity in range(2):
            values = jnp.dot(
                proj_t[width : 2 * width, 0:depth], fields[parity], preferred_element_type=F32
            )
            term = values.reshape(heads, size, pairs) * weights[parity][:, None, :]
            mixed = term if mixed is None else mixed + term
        mixed = mixed.reshape(width, pairs).astype(BF16)
        added = lax.dot_general(mixed, chosen, NT, preferred_element_type=F32)
        acc[...] = (
            acc[...].reshape(heads, size, rows) * factor[:, None, :]
        ).reshape(width, rows) + added
        return carry

    lax.fori_loop(0, Z, group_step, 0)

    scale = 1.0 / total_ref[...]
    encoded = (acc[...].reshape(heads, size, rows) * scale[:, None, :]).reshape(width, rows)
    hidden = latent_ref[...].astype(F32) + encoded.T
    hidden_ref[...] = hidden
    center = hidden - jnp.mean(hidden, axis=1, keepdims=True)
    variance = jnp.mean(center * center, axis=1, keepdims=True)
    extended[reach : reach + rows, :] = (
        center * lax.rsqrt(variance + 1e-05) * gain_ref[...]
    ).astype(BF16)

    def halo_copy(which, there, here, to):
        return pltpu.make_async_remote_copy(
            src_ref=extended.at[there], dst_ref=extended.at[here],
            send_sem=halo_send.at[which], recv_sem=halo_recv.at[which],
            device_id=(y, to), device_id_type=MESH,
        )

    up = halo_copy(0, pl.ds(rows, reach), pl.ds(0, reach), (seq + 1) % owners)
    down = halo_copy(
        1, pl.ds(reach, reach), pl.ds(reach + rows, reach), (seq + owners - 1) % owners
    )
    pl.when(seq < last)(up.start)
    pl.when(seq > 0)(down.start)

    tile = 512
    for fetch in fetches:
        fetch.wait()

    def own_tile(index, carry):
        at = pl.ds(pl.multiple_of(index * tile, tile), tile)
        found = jnp.dot(
            extended[reach : reach + rows, :], big[:, at], preferred_element_type=F32
        )
        scaling = jnp.where(index * tile < width, size ** -0.5, 1.0)
        mixed_rows[reach : reach + rows, at] = (found * scaling).astype(BF16)
        return carry

    lax.fori_loop(0, 3 * width // tile, own_tile, 0)
    pl.when(seq > 0)(up.wait_recv)
    pl.when(seq < last)(down.wait_recv)

    def halo_tile(index, carry):
        at = pl.ds(pl.multiple_of(index * tile + width, tile), tile)
        both = jnp.concatenate([extended[0:reach, :], extended[reach + rows :, :]], axis=0)
        found = jnp.dot(both, big[:, at], preferred_element_type=F32).astype(BF16)
        mixed_rows[0:reach, at] = found[0:reach]
        mixed_rows[reach + rows :, at] = found[reach:]
        return carry

    lax.fori_loop(0, 2 * width // tile, halo_tile, 0)

    def place(y_to, x_to, z_to, core_to):
        return (y_to, x_to * (Z * CORES) + z_to * CORES + core_to)

    def remote(src_ref, dst_ref, send_sem, recv_sem, peer):
        return pltpu.make_async_remote_copy(
            src_ref=src_ref, dst_ref=dst_ref, send_sem=send_sem, recv_sem=recv_sem,
            device_id=peer, device_id_type=MESH,
        )

    part_width = width // X
    half_width = width // 2
    strip_width = half_width // Y

    def strip(who):
        return pl.ds(pl.multiple_of(half_width + who * strip_width, strip_width), strip_width)

    def part_of(turn):
        return (x + 1 + turn) % X

    def core_copy(turn):
        part = part_of(turn)
        return remote(
            grads.at[part, :, 1 - core], from_core.at[part], core_send.at[part],
            core_recv.at[part], place(y, x, z, 1 - core),
        )

    def x_copy(turn):
        part = part_of(turn)
        return remote(
            merged.at[part, :, :, pl.ds(0, half_width)], x_in.at[turn], x_send.at[turn],
            x_recv.at[turn], place(y, part, z, core),
        )

    def y_copy(turn, k):
        part = part_of(turn)
        return remote(
            merged.at[part, :, :, strip((y + k) % Y)], v_in.at[k - 1, part],
            y_send.at[k - 1, part], y_recv.at[k - 1, part], y_peers[k - 1],
        )

    def pass_part(turn, with_x):
        part = part_of(turn)
        core_copy(turn).wait_recv()
        merged[part] = (
            grads[part, :, core].astype(F32) + from_core[part].astype(F32)
        ).astype(BF16)
        for k in range(1, Y):
            y_copy(turn, k).start()
        if with_x:
            x_copy(turn).start()

    def part_step(turn, carry):
        part = part_of(turn)

        def columns(base):
            return pl.ds(pl.multiple_of(base + part * part_width, part_width), part_width)

        for block in range(2):
            mine = slice((block + 1) * reach, (block + 2) * reach)
            theirs = slice(block * reach, block * reach + span)
            queries = mixed_rows[mine, columns(0)]
            keys = mixed_rows[theirs, columns(width)]
            values = mixed_rows[theirs, columns(2 * width)]
            made = []
            for head in range(heads // X):
                here = slice(head * size, (head + 1) * size)
                logits = lax.dot_general(
                    queries[:, here], keys[:, here], NT, preferred_element_type=F32
                ) + tables[block, part * (heads // X) + head]
                powered = jnp.exp(logits - jnp.max(logits, axis=1, keepdims=True))
                total = jnp.sum(powered, axis=1, keepdims=True)
                mixture = jnp.dot(
                    powered.astype(BF16), values[:, here], preferred_element_type=F32
                )
                made.append((mixture / total).astype(BF16))
            attended[block * reach : (block + 1) * reach, columns(0)] = jnp.concatenate(
                made, axis=1
            )
        found = lax.dot_general(
            attended[:, columns(0)], cotangent[0], TN, preferred_element_type=F32
        )
        grads[part] = found.astype(BF16).reshape(Z, CORES, 16, width)
        core_copy(turn).start()

        @pl.when(turn > 0)
        def pass_earlier():
            pass_part(turn - 1, True)

        return carry

    lax.fori_loop(0, X, part_step, 0)
    pass_part(X - 1, False)

    def out_tile(index, carry):
        at = pl.ds(pl.multiple_of(index * tile, tile), tile)
        processed_ref[:, at] = (
            hidden_ref[:, at]
            + jnp.dot(attended[...], out_proj[:, at], preferred_element_type=F32)
        ).astype(BF16)
        return carry

    lax.fori_loop(0, width // tile, out_tile, 0)

    z_peers = [place(y, x, (z + k) % Z, core) for k in range(1, Z)]
    x_peers = [place(y, (x + k) % X, z, core) for k in range(1, X)]
    for turn in range(X - 1):
        x_copy(turn).wait_recv()
    x_sum[...] = (
        merged[x, :, :, 0:half_width].astype(F32)
        + (x_in[0].astype(F32) + x_in[1].astype(F32) + x_in[2].astype(F32))
    ).astype(BF16)
    z_copies = [
        remote(x_sum.at[(z + k) % Z], z_in.at[k - 1], z_send.at[k - 1], z_recv.at[k - 1], z_peers[k - 1])
        for k in range(1, Z)
    ]
    for copy in z_copies:
        copy.start()
    for turn in range(X):
        for k in range(1, Y):
            y_copy(turn, k).wait_recv()
    v_sum[...] = (
        merged[:, :, :, strip(y)].astype(F32)
        + (v_in[0].astype(F32) + v_in[1].astype(F32) + v_in[2].astype(F32))
    ).astype(BF16)
    u_copies = [
        remote(v_sum.at[(x + k) % X], u_in.at[k - 1], u_send.at[k - 1], u_recv.at[k - 1], x_peers[k - 1])
        for k in range(1, X)
    ]
    for copy in u_copies:
        copy.start()
    for copy in z_copies:
        copy.wait_recv()
    found = x_sum[z].astype(F32)
    for k in range(Z - 1):
        found = found + z_in[k].astype(F32)
    y_all[y] = found
    s_copies = [
        remote(y_all.at[y], y_all.at[y], s_send.at[k - 1], s_recv.at[k - 1], y_peers[k - 1])
        for k in range(1, Y)
    ]
    for copy in s_copies:
        copy.start()
    for copy in u_copies:
        copy.wait_recv()
    u_sum[...] = (
        v_sum[x].astype(F32)
        + (u_in[0].astype(F32) + u_in[1].astype(F32) + u_in[2].astype(F32))
    ).astype(BF16)
    w_copies = [
        remote(u_sum.at[(z + k) % Z], w_in.at[k - 1], w_send.at[k - 1], w_recv.at[k - 1], z_peers[k - 1])
        for k in range(1, Z)
    ]
    for copy in w_copies:
        copy.start()
    for copy in w_copies:
        copy.wait_recv()
    found = u_sum[z].astype(F32)
    for k in range(Z - 1):
        found = found + w_in[k].astype(F32)
    r_all[y] = found
    r_copies = [
        remote(r_all.at[y], r_all.at[y], r_send.at[k - 1], r_recv.at[k - 1], y_peers[k - 1])
        for k in range(1, Y)
    ]
    for copy in r_copies:
        copy.start()
    for copy in s_copies:
        copy.wait_recv()
    gradient_ref[:, 0:half_width] = (y_all[0] + y_all[1]) + (y_all[2] + y_all[3])
    for copy in r_copies:
        copy.wait_recv()
    for k in range(Y):
        at = half_width + k * strip_width
        gradient_ref[:, at : at + strip_width] = r_all[k]

    def sent_step(step, carry):
        to, copy = block_copy(step)

        @pl.when(to != seq)
        def done():
            copy.wait_send()

        return carry

    lax.fori_loop(0, owners, sent_step, 0)
    pl.when(seq < last)(up.wait_send)
    pl.when(seq > 0)(down.wait_send)
    for turn in range(X):
        core_copy(turn).wait_send()
        for k in range(1, Y):
            y_copy(turn, k).wait_send()
    for turn in range(X - 1):
        x_copy(turn).wait_send()
    for copy in z_copies + u_copies + s_copies + w_copies + r_copies:
        copy.wait_send()


def shards(
    grid_fields, mesh_latent, edge_source, edge_target, edge_count, edge_bias, encoder_proj,
    norm_gain, processor_proj, offset_bias, windows, output_proj, cotangent,
):
    shard_count = lax.axis_size("seq")
    device = lax.axis_index("seq")
    rows, width = mesh_latent.shape
    heads = offset_bias.shape[0]
    reach = (offset_bias.shape[1] - 1) // 2
    channels, points = grid_fields.shape[1:]
    capacity = edge_source.shape[2]
    offset = jnp.arange(3 * reach, dtype=jnp.int32) - reach
    table = jnp.where(
        jnp.abs(offset)[None, :] <= windows[:, None],
        jnp.pad(offset_bias, ((0, 0), (0, reach - 1))),
        NEG,
    )
    depth = (channels + 15) // 16 * 16
    chips = shard_count // CORES
    strip_width = width // 2 // Y
    dma = pltpu.SemaphoreType.DMA
    hbm = pl.BlockSpec(memory_space=pltpu.HBM)
    processed, gradient = pl.pallas_call(
        layer_kernel,
        out_shape=(
            jax.ShapeDtypeStruct((rows, width), BF16),
            jax.ShapeDtypeStruct((16, width), F32),
        ),
        in_specs=[pl.BlockSpec(memory_space=pltpu.SMEM)] + [vmem()] * 8 + [hbm] * 3,
        out_specs=(vmem(), vmem()),
        scratch_shapes=[
            pltpu.VMEM((points, 128), F32),
            pltpu.VMEM((128, 128), F32),
            pltpu.VMEM((shard_count, depth, capacity), BF16),
            pltpu.VMEM((shard_count, depth, capacity), BF16),
            pltpu.VMEM((width, rows), BF16),
            pltpu.VMEM((2 * width, 128), BF16),
            pltpu.VMEM((shard_count, capacity), jnp.int32),
            pltpu.VMEM((chips, capacity), jnp.int32),
            pltpu.VMEM((2, chips, capacity), F32),
            pltpu.VMEM((width, rows), F32),
            pltpu.VMEM((heads, rows), F32),
            pltpu.VMEM((heads, rows), F32),
            dma((shard_count,)),
            dma((shard_count,)),
            pltpu.VMEM((width, 3 * width), BF16),
            pltpu.VMEM((width, width), BF16),
            pltpu.VMEM((1, rows, width), BF16),
            dma((3,)),
            pltpu.VMEM((rows, width), F32),
            pltpu.VMEM((rows + 2 * reach, width), BF16),
            pltpu.VMEM((rows + 2 * reach, 3 * width), BF16),
            pltpu.VMEM((2, heads, reach, 3 * reach), F32),
            pltpu.VMEM((rows, width), BF16),
            dma((2,)),
            dma((2,)),
            pltpu.VMEM((X, Z, CORES, 16, width), BF16),
            pltpu.VMEM((X, Z, 16, width), BF16),
            pltpu.VMEM((X, Z, 16, width), BF16),
            pltpu.VMEM((X - 1, Z, 16, width // 2), BF16),
            pltpu.VMEM((Z, 16, width // 2), BF16),
            pltpu.VMEM((Z - 1, 16, width // 2), BF16),
            pltpu.VMEM((Y, 16, width // 2), F32),
            pltpu.VMEM((Y - 1, X, Z, 16, strip_width), BF16),
            pltpu.VMEM((X, Z, 16, strip_width), BF16),
            pltpu.VMEM((X - 1, Z, 16, strip_width), BF16),
            pltpu.VMEM((Z, 16, strip_width), BF16),
            pltpu.VMEM((Z - 1, 16, strip_width), BF16),
            pltpu.VMEM((Y, 16, strip_width), F32),
            dma((X,)),
            dma((X,)),
            dma((X - 1,)),
            dma((X - 1,)),
            dma((Y - 1, X)),
            dma((Y - 1, X)),
            dma((Z - 1,)),
            dma((Z - 1,)),
            dma((Y - 1,)),
            dma((Y - 1,)),
            dma((X - 1,)),
            dma((X - 1,)),
            dma((Z - 1,)),
            dma((Z - 1,)),
            dma((Y - 1,)),
            dma((Y - 1,)),
        ],
        compiler_params=pltpu.CompilerParams(
            vmem_limit_bytes=VMEM_LIMIT, collective_id=2, has_side_effects=True
        ),
        name="layer",
    )(
        edge_source[0], grid_fields, edge_target[0], edge_count, edge_bias[0], mesh_latent,
        encoder_proj, norm_gain[None], table, processor_proj, output_proj, cotangent,
    )

    return (processed[None], gradient)


def solution(mesh):
    in_specs = (
        P("dp", None, "seq"),
        P("seq", None),
        P("seq", None, None),
        P("seq", None, None),
        P(),
        P("seq", None, None),
        P(),
        P(),
        P(),
        P(),
        P(),
        P(),
        P("dp", "seq", None),
    )
    out_specs = (P("dp", "seq", None), P("seq", None))
    return jax.shard_map(shards, mesh=mesh, in_specs=in_specs, out_specs=out_specs, check_vma=False)
```

```python
import jax
import jax.numpy as jnp
from jax import lax
from jax.experimental import pallas as pl
from jax.experimental.pallas import tpu as pltpu
from jax.sharding import PartitionSpec as P

MESH = pl.DeviceIdType.MESH
X, Z, CORES, Y = 4, 8, 2, 4
UNITS = 4
NEG = -1e30
F32 = jnp.float32
BF16 = jnp.bfloat16
VMEM_LIMIT = 56 * 1024 * 1024

NT = (((1,), (1,)), ((), ()))
TN = (((0,), (0,)), ((), ()))


def vmem():
    return pl.BlockSpec(memory_space=pltpu.VMEM)


def layer_kernel(
    source_ref, windows_ref, grid_ref, target_ref, count_ref, bias_ref, latent_ref, proj_ref,
    gain_ref, offset_ref, big_hbm, out_hbm, cotangent_hbm,
    processed_ref, gradient_ref, table, stage, outgoing, incoming, latent_t, proj_t, counts,
    targets, biases, acc, peak_ref, total_ref, send, recv,
    big, out_proj, cotangent, fetched, hidden_ref, extended, mixed_rows, offsets, tables,
    attended_t, attended, halo_send, halo_recv, grads, from_core, merged, v_in, v_sum, w_in,
    r_all, core_send, core_recv, y_send, y_recv, w_send, w_recv, r_send, r_recv,
):
    seq = lax.axis_index("seq")
    y = lax.axis_index("dp")
    core = seq % CORES
    z = (seq // CORES) % Z
    x = seq // (CORES * Z)
    channels = grid_ref.shape[1]
    owners, capacity = source_ref.shape
    rows, width = latent_ref.shape
    heads = peak_ref.shape[0]
    size = width // heads
    half = capacity // 2
    group = CORES * UNITS
    depth = outgoing.shape[1]

    def shifts(turn, chip_at):
        pair_at, unit = turn * (UNITS // 2) + chip_at // 2, chip_at % 2
        lap, leg = pair_at // 4, pair_at % 4
        x_shift = 2 + (1 - 2 * (lap % 2)) * ((lap + 1) // 2)
        z_shift = (1 - unit) * (4 - leg) + unit * (leg + 4 * ((leg + 3) // 4))
        return x_shift, z_shift

    barrier = pltpu.get_barrier_semaphore()

    def greet(offset, carry):
        pl.semaphore_signal(
            barrier, inc=1, device_id=(y, (seq + offset) % owners), device_id_type=MESH
        )
        return carry

    lax.fori_loop(1, owners, greet, 0)
    y_peers = [((y + k) % Y, seq) for k in range(1, Y)]
    for peer in y_peers:
        pl.semaphore_signal(barrier, inc=1, device_id=peer, device_id_type=MESH)
    fetches = [
        pltpu.make_async_copy(big_hbm, big, fetched.at[0]),
        pltpu.make_async_copy(out_hbm, out_proj, fetched.at[1]),
        pltpu.make_async_copy(cotangent_hbm, cotangent, fetched.at[2]),
    ]
    for fetch in fetches:
        fetch.start()
    stage[...] = jnp.zeros_like(stage)

    def turn_fields(chunk, carry):
        start = pl.multiple_of(chunk * 128, 128)
        stage[0:channels, :] = grid_ref[0, :, pl.ds(start, 128)].astype(F32)
        table[pl.ds(start, 128), :] = stage[...].T
        return carry

    lax.fori_loop(0, grid_ref.shape[2] // 128, turn_fields, 0)
    pl.semaphore_wait(barrier, owners - 1 + Y - 1)

    def block_copy(step):
        x_shift, z_shift = shifts(step // group, (step // CORES) % UNITS)
        to_x = (x + x_shift) % X
        to_z = (z + z_shift) % Z
        to = to_x * (Z * CORES) + to_z * CORES + step % CORES
        slot = step - step % CORES + core
        copy = pltpu.make_async_remote_copy(
            src_ref=outgoing.at[step], dst_ref=incoming.at[slot],
            send_sem=send.at[step], recv_sem=recv.at[slot],
            device_id=(y, to), device_id_type=MESH,
        )
        return to, copy

    def send_step(step, carry):
        to, copy = block_copy(step)
        for slot in range(capacity):
            row = (slot % 2) * half + slot // 2
            stage[row : row + 1, :] = table[pl.ds(source_ref[to, slot], 1), :]
        block = stage[...].T[0:depth, :].astype(BF16)

        @pl.when(to == seq)
        def keep():
            incoming[step] = block

        @pl.when(to != seq)
        def pass_on():
            outgoing[step] = block
            copy.start()

        return carry

    lax.fori_loop(0, owners, send_step, 0)

    for chunk in range(width // 128):
        here = slice(chunk * 128, (chunk + 1) * 128)
        latent_t[here, :] = latent_ref[:, here].astype(F32).T.astype(BF16)
    stage[...] = jnp.zeros_like(stage)

    def turn_proj(chunk, carry):
        start = pl.multiple_of(chunk * 128, 128)
        stage[0:channels, :] = proj_ref[:, pl.ds(start, 128)].astype(F32)
        proj_t[pl.ds(start, 128), :] = stage[...].T.astype(BF16)
        return carry

    lax.fori_loop(0, 2 * width // 128, turn_proj, 0)

    chips = owners // CORES
    lane = lax.broadcasted_iota(jnp.int32, (chips, capacity), 1)
    slot_row = lax.broadcasted_iota(jnp.int32, (capacity, capacity), 0)
    slot_lane = lax.broadcasted_iota(jnp.int32, (capacity, capacity), 1)
    owner_lane = lax.broadcasted_iota(jnp.int32, (owners, owners), 1)
    own = jnp.sum(jnp.where(owner_lane == seq, count_ref[...], 0), axis=1, keepdims=True)
    counts[...] = jnp.broadcast_to(own, (owners, capacity))

    def of_core(ref, which):
        return ref[pl.ds(which, chips, stride=CORES), :]

    def picks(parity, which):
        wanted = slot_row == 2 * (slot_lane - which * half) + parity
        in_half = (slot_lane >= which * half) & (slot_lane < (which + 1) * half)
        return jnp.where(wanted & in_half, 1.0, 0.0)

    found = jnp.zeros((chips, capacity), F32)
    for which in range(CORES):
        found = found + jnp.dot(
            of_core(target_ref, which).astype(F32), picks(0, which),
            precision=lax.Precision.HIGHEST, preferred_element_type=F32,
        )
    targets[...] = found.astype(jnp.int32)
    live = jnp.where(lane < half, of_core(counts, 0), of_core(counts, 1))
    for parity in range(2):
        found = jnp.zeros((chips, capacity), F32)
        for which in range(CORES):
            found = found + jnp.dot(
                of_core(bias_ref, which), picks(parity, which),
                precision=lax.Precision.HIGHEST, preferred_element_type=F32,
            )
        biases[parity] = jnp.where(2 * (lane % half) + parity < live, found, NEG)

    span, reach = tables.shape[2], tables.shape[3] // 2
    last = owners - 1

    @pl.when(seq == 0)
    def no_before():
        extended[0:reach, :] = jnp.zeros((reach, width), BF16)

    @pl.when(seq == last)
    def no_after():
        extended[reach + rows :, :] = jnp.zeros((reach, width), BF16)

    offsets[...] = jnp.zeros_like(offsets)
    offsets[:, 0 : 2 * reach + 1] = offset_ref[...]
    key_lane = lax.broadcasted_iota(jnp.int32, (1, span), 1)
    key_row = lax.broadcasted_iota(jnp.int32, (span, reach), 0)
    edges = [
        jnp.where((key_row < reach) & (seq == 0), NEG, 0.0),
        jnp.where((key_row >= 2 * reach) & (seq == last), NEG, 0.0),
    ]

    def table_step(pair, carry):
        for side in range(2):
            head = pair * 2 + side
            row = jnp.where(
                jnp.abs(key_lane - reach) <= windows_ref[head], offsets[pl.ds(head, 1), :], NEG
            )
            row = jnp.broadcast_to(row, (reach, span))
            spread = pltpu.roll(row, 0, 1, stride=1, stride_axis=0).T
            for block in range(2):
                tables[block, pair, :, side * reach : (side + 1) * reach] = spread + edges[block]
        return carry

    lax.fori_loop(0, heads // 2, table_step, 0)

    acc[...] = jnp.zeros_like(acc)
    peak_ref[...] = jnp.zeros_like(peak_ref)
    total_ref[...] = jnp.ones_like(total_ref)
    pairs = UNITS * capacity
    low = lax.broadcasted_iota(jnp.int32, (depth, capacity), 1) < half
    peak_lane = lax.broadcasted_iota(jnp.int32, (rows, 128), 1)
    row_index = lax.broadcasted_iota(jnp.int32, (rows, pairs), 0)

    def group_step(turn, carry):
        for member_at in range(group):
            slot = turn * group + member_at

            @pl.when(slot != 25 * CORES + core)
            def arrive():
                pltpu.make_async_copy(
                    incoming.at[slot], incoming.at[slot], recv.at[slot]
                ).wait()

        evens, odds, rows_of, bias_of = [], [], [], [[], []]
        for unit in range(UNITS):
            first = incoming[turn * group + CORES * unit].astype(F32)
            second = incoming[turn * group + CORES * unit + 1].astype(F32)
            evens.append(jnp.where(low, first, pltpu.roll(second, half, 1)).astype(BF16))
            odds.append(jnp.where(low, pltpu.roll(first, half, 1), second).astype(BF16))
            x_shift, z_shift = shifts(turn, unit)
            chip = ((x + X - x_shift) % X) * Z + (z + Z - z_shift) % Z
            rows_of.append(targets[pl.ds(chip, 1), :])
            for parity in range(2):
                bias_of[parity].append(biases[parity, pl.ds(chip, 1), :])
        target = jnp.concatenate(rows_of, axis=1)
        member = row_index == target
        chosen = jnp.where(member, 1.0, 0.0).astype(BF16)
        queries = jnp.dot(latent_t[...], chosen, preferred_element_type=F32)
        scores, fields = [], []
        for parity, parts in enumerate((evens, odds)):
            part = jnp.concatenate(parts, axis=1)
            keys = jnp.dot(proj_t[0:width, 0:depth], part, preferred_element_type=F32)
            logits = jnp.sum((queries * keys).reshape(heads, size, pairs), axis=1)
            scores.append(logits * (size ** -0.5) + jnp.concatenate(bias_of[parity], axis=1))
            fields.append(part)
        pair_peak = jnp.maximum(scores[0], scores[1])
        peaks = jnp.full((rows, 128), NEG, F32)
        for head in range(heads):
            column = jnp.max(
                jnp.where(member, pair_peak[head : head + 1, :], NEG), axis=1, keepdims=True
            )
            peaks = jnp.where(peak_lane == head, column, peaks)
        old = peak_ref[...]
        new = jnp.maximum(old, peaks.T[0:heads, :])
        upper = new.astype(BF16)
        lower = (new - upper.astype(F32)).astype(BF16)
        new = upper.astype(F32) + lower.astype(F32)
        peak_ref[...] = new
        factor = jnp.exp(old - new)
        slot_peak = jnp.dot(upper, chosen, preferred_element_type=F32) + jnp.dot(
            lower, chosen, preferred_element_type=F32
        )
        weights = [jnp.exp(score - slot_peak) for score in scores]
        both = weights[0] + weights[1]
        both_upper = both.astype(BF16)
        both_lower = (both - both_upper.astype(F32)).astype(BF16)
        sums = lax.dot_general(both_upper, chosen, NT, preferred_element_type=F32)
        sums = sums + lax.dot_general(both_lower, chosen, NT, preferred_element_type=F32)
        total_ref[...] = total_ref[...] * factor + sums
        mixed = None
        for parity in range(2):
            values = jnp.dot(
                proj_t[width : 2 * width, 0:depth], fields[parity], preferred_element_type=F32
            )
            term = values.reshape(heads, size, pairs) * weights[parity][:, None, :]
            mixed = term if mixed is None else mixed + term
        mixed = mixed.reshape(width, pairs).astype(BF16)
        added = lax.dot_general(mixed, chosen, NT, preferred_element_type=F32)
        acc[...] = (
            acc[...].reshape(heads, size, rows) * factor[:, None, :]
        ).reshape(width, rows) + added
        return carry

    lax.fori_loop(0, owners // group, group_step, 0)

    scale = 1.0 / total_ref[...]
    encoded = (acc[...].reshape(heads, size, rows) * scale[:, None, :]).reshape(width, rows)
    hidden = latent_ref[...].astype(F32) + encoded.T
    hidden_ref[...] = hidden
    center = hidden - jnp.mean(hidden, axis=1, keepdims=True)
    variance = jnp.mean(center * center, axis=1, keepdims=True)
    extended[reach : reach + rows, :] = (
        center * lax.rsqrt(variance + 1e-05) * gain_ref[...]
    ).astype(BF16)

    def halo_copy(which, there, here, to):
        return pltpu.make_async_remote_copy(
            src_ref=extended.at[there], dst_ref=extended.at[here],
            send_sem=halo_send.at[which], recv_sem=halo_recv.at[which],
            device_id=(y, to), device_id_type=MESH,
        )

    up = halo_copy(0, pl.ds(rows, reach), pl.ds(0, reach), (seq + 1) % owners)
    down = halo_copy(
        1, pl.ds(reach, reach), pl.ds(reach + rows, reach), (seq + owners - 1) % owners
    )
    pl.when(seq < last)(up.start)
    pl.when(seq > 0)(down.start)

    tile = 512
    for fetch in fetches:
        fetch.wait()

    def own_tile(index, carry):
        at = pl.ds(pl.multiple_of(index * tile, tile), tile)
        found = jnp.dot(
            extended[reach : reach + rows, :], big[:, at], preferred_element_type=F32
        )
        scaling = jnp.where(index * tile < width, size ** -0.5, 1.0)
        mixed_rows[reach : reach + rows, at] = (found * scaling).astype(BF16)
        return carry

    lax.fori_loop(0, 3 * width // tile, own_tile, 0)
    pl.when(seq > 0)(up.wait_recv)
    pl.when(seq < last)(down.wait_recv)

    def halo_tile(index, carry):
        at = pl.ds(pl.multiple_of(index * tile + width, tile), tile)
        both = jnp.concatenate([extended[0:reach, :], extended[reach + rows :, :]], axis=0)
        found = jnp.dot(both, big[:, at], preferred_element_type=F32).astype(BF16)
        mixed_rows[0:reach, at] = found[0:reach]
        mixed_rows[reach + rows :, at] = found[reach:]
        return carry

    lax.fori_loop(0, 2 * width // tile, halo_tile, 0)

    def place(y_to, x_to, z_to, core_to):
        return (y_to, x_to * (Z * CORES) + z_to * CORES + core_to)

    def remote(src_ref, dst_ref, send_sem, recv_sem, peer):
        return pltpu.make_async_remote_copy(
            src_ref=src_ref, dst_ref=dst_ref, send_sem=send_sem, recv_sem=recv_sem,
            device_id=peer, device_id_type=MESH,
        )

    part_width = width // X
    strip_width = width // Y

    def strip(who):
        return pl.ds(pl.multiple_of(who * strip_width, strip_width), strip_width)

    def part_of(turn):
        return (x + 1 + turn) % X

    def core_copy(turn):
        part = part_of(turn)
        return remote(
            grads.at[part, :, 1 - core], from_core.at[part], core_send.at[part],
            core_recv.at[part], place(y, x, z, 1 - core),
        )

    def y_copy(turn, k):
        part = part_of(turn)
        return remote(
            merged.at[part, :, :, strip((y + k) % Y)], v_in.at[k - 1, part],
            y_send.at[k - 1, part], y_recv.at[k - 1, part], y_peers[k - 1],
        )

    def w_copy(turn, k):
        part = part_of(turn)
        to_z = (z + k) % Z
        return remote(
            v_sum.at[part, to_z], w_in.at[turn, k], w_send.at[turn, k], w_recv.at[turn, k],
            place(y, part, to_z, core),
        )

    def pass_to_y(turn):
        part = part_of(turn)
        core_copy(turn).wait_recv()
        merged[part] = (
            grads[part, :, core].astype(F32) + from_core[part].astype(F32)
        ).astype(BF16)
        for k in range(1, Y):
            y_copy(turn, k).start()

    def pass_to_owners(turn, first):
        part = part_of(turn)
        for k in range(1, Y):
            y_copy(turn, k).wait_recv()
        v_sum[part] = (
            merged[part, :, :, strip(y)].astype(F32)
            + (v_in[0, part].astype(F32) + v_in[1, part].astype(F32) + v_in[2, part].astype(F32))
        ).astype(BF16)
        for k in range(first, Z):
            w_copy(turn, k).start()

    side_lane = lax.broadcasted_iota(jnp.int32, (reach, 2 * size), 1) < size

    def part_step(turn, carry):
        part = part_of(turn)

        def columns(base, pair):
            at = base + part * part_width + pair * 2 * size
            return pl.ds(pl.multiple_of(at, 2 * size), 2 * size)

        pairs_in_part = part_width // (2 * size)
        for block in range(2):
            mine = slice((block + 1) * reach, (block + 2) * reach)
            theirs = slice(block * reach, block * reach + span)
            for pair in range(pairs_in_part):
                queries = mixed_rows[mine, columns(0, pair)]
                none = jnp.zeros_like(queries)
                queries = jnp.concatenate(
                    [jnp.where(side_lane, queries, none), jnp.where(side_lane, none, queries)],
                    axis=0,
                )
                logits = lax.dot_general(
                    mixed_rows[theirs, columns(width, pair)], queries, NT,
                    preferred_element_type=F32,
                ) + tables[block, part * pairs_in_part + pair]
                powered = jnp.exp(logits - jnp.max(logits, axis=0, keepdims=True))
                scale = 1.0 / jnp.sum(powered, axis=0, keepdims=True)
                mixture = lax.dot_general(
                    mixed_rows[theirs, columns(2 * width, pair)], powered.astype(BF16), TN,
                    preferred_element_type=F32,
                ) * scale
                across = slice(block * reach, (block + 1) * reach)
                for side in range(2):
                    down_at = part * part_width + (pair * 2 + side) * size
                    attended_t[pl.ds(pl.multiple_of(down_at, size), size), across] = mixture[
                        side * size : (side + 1) * size, side * reach : (side + 1) * reach
                    ].astype(BF16)
        found = jnp.dot(
            attended_t[pl.ds(pl.multiple_of(part * part_width, part_width), part_width), :],
            cotangent[0], preferred_element_type=F32,
        )
        grads[part] = found.astype(BF16).reshape(Z, CORES, 16, width)
        core_copy(turn).start()

        @pl.when(turn > 0)
        def pass_one():
            pass_to_y(turn - 1)

        @pl.when(turn > 1)
        def pass_two():
            pass_to_owners(turn - 2, 0)

        return carry

    lax.fori_loop(0, X, part_step, 0)
    pass_to_owners(X - 2, 0)
    attended[...] = attended_t[...].astype(F32).T.astype(BF16)

    def out_tile(index):
        at = slice(index * tile, (index + 1) * tile)
        processed_ref[:, at] = (
            hidden_ref[:, at]
            + jnp.dot(attended[...], out_proj[:, at], preferred_element_type=F32)
        ).astype(BF16)

    pass_to_y(X - 1)
    for index in range(width // tile):
        out_tile(index)
    pass_to_owners(X - 1, 1)
    total = v_sum[x, z].astype(F32)
    for turn in range(X):
        for k in range(1 if turn == X - 1 else 0, Z):
            w_copy(turn, k).wait_recv()
            total = total + w_in[turn, k].astype(F32)
    r_all[y] = total
    r_copies = [
        remote(r_all.at[y], r_all.at[y], r_send.at[k - 1], r_recv.at[k - 1], y_peers[k - 1])
        for k in range(1, Y)
    ]
    for copy in r_copies:
        copy.start()

    def sent_step(step, carry):
        to, copy = block_copy(step)

        @pl.when(to != seq)
        def done():
            copy.wait_send()

        return carry

    lax.fori_loop(0, owners, sent_step, 0)
    pl.when(seq < last)(up.wait_send)
    pl.when(seq > 0)(down.wait_send)
    for turn in range(X):
        core_copy(turn).wait_send()
        for k in range(1, Y):
            y_copy(turn, k).wait_send()
        for k in range(1 if turn == X - 1 else 0, Z):
            w_copy(turn, k).wait_send()
    for copy in r_copies:
        copy.wait_recv()
    for k in range(Y):
        gradient_ref[:, k * strip_width : (k + 1) * strip_width] = r_all[k]
    for copy in r_copies:
        copy.wait_send()


def shards(
    grid_fields, mesh_latent, edge_source, edge_target, edge_count, edge_bias, encoder_proj,
    norm_gain, processor_proj, offset_bias, windows, output_proj, cotangent,
):
    shard_count = lax.axis_size("seq")
    device = lax.axis_index("seq")
    rows, width = mesh_latent.shape
    heads = offset_bias.shape[0]
    reach = (offset_bias.shape[1] - 1) // 2
    channels, points = grid_fields.shape[1:]
    capacity = edge_source.shape[2]
    depth = (channels + 15) // 16 * 16
    chips = shard_count // CORES
    strip_width = width // Y
    dma = pltpu.SemaphoreType.DMA
    hbm = pl.BlockSpec(memory_space=pltpu.HBM)
    processed, gradient = pl.pallas_call(
        layer_kernel,
        out_shape=(
            jax.ShapeDtypeStruct((rows, width), BF16),
            jax.ShapeDtypeStruct((16, width), F32),
        ),
        in_specs=[pl.BlockSpec(memory_space=pltpu.SMEM)] * 2 + [vmem()] * 8 + [hbm] * 3,
        out_specs=(vmem(), vmem()),
        scratch_shapes=[
            pltpu.VMEM((points, 128), F32),
            pltpu.VMEM((128, 128), F32),
            pltpu.VMEM((shard_count, depth, capacity), BF16),
            pltpu.VMEM((shard_count, depth, capacity), BF16),
            pltpu.VMEM((width, rows), BF16),
            pltpu.VMEM((2 * width, 128), BF16),
            pltpu.VMEM((shard_count, capacity), jnp.int32),
            pltpu.VMEM((chips, capacity), jnp.int32),
            pltpu.VMEM((2, chips, capacity), F32),
            pltpu.VMEM((width, rows), F32),
            pltpu.VMEM((heads, rows), F32),
            pltpu.VMEM((heads, rows), F32),
            dma((shard_count,)),
            dma((shard_count,)),
            pltpu.VMEM((width, 3 * width), BF16),
            pltpu.VMEM((width, width), BF16),
            pltpu.VMEM((1, rows, width), BF16),
            dma((3,)),
            pltpu.VMEM((rows, width), F32),
            pltpu.VMEM((rows + 2 * reach, width), BF16),
            pltpu.VMEM((rows + 2 * reach, 3 * width), BF16),
            pltpu.VMEM((heads, 3 * reach), F32),
            pltpu.VMEM((2, heads // 2, 3 * reach, 2 * reach), F32),
            pltpu.VMEM((width, rows), BF16),
            pltpu.VMEM((rows, width), BF16),
            dma((2,)),
            dma((2,)),
            pltpu.VMEM((X, Z, CORES, 16, width), BF16),
            pltpu.VMEM((X, Z, 16, width), BF16),
            pltpu.VMEM((X, Z, 16, width), BF16),
            pltpu.VMEM((Y - 1, X, Z, 16, strip_width), BF16),
            pltpu.VMEM((X, Z, 16, strip_width), BF16),
            pltpu.VMEM((X, Z, 16, strip_width), BF16),
            pltpu.VMEM((Y, 16, strip_width), F32),
            dma((X,)),
            dma((X,)),
            dma((Y - 1, X)),
            dma((Y - 1, X)),
            dma((X, Z)),
            dma((X, Z)),
            dma((Y - 1,)),
            dma((Y - 1,)),
        ],
        compiler_params=pltpu.CompilerParams(
            vmem_limit_bytes=VMEM_LIMIT, collective_id=2, has_side_effects=True
        ),
        name="layer",
    )(
        edge_source[0], windows, grid_fields, edge_target[0], edge_count, edge_bias[0], mesh_latent,
        encoder_proj, norm_gain[None], offset_bias, processor_proj, output_proj, cotangent,
    )

    return (processed[None], gradient)


def solution(mesh):
    in_specs = (
        P("dp", None, "seq"),
        P("seq", None),
        P("seq", None, None),
        P("seq", None, None),
        P(),
        P("seq", None, None),
        P(),
        P(),
        P(),
        P(),
        P(),
        P(),
        P("dp", "seq", None),
    )
    out_specs = (P("dp", "seq", None), P("seq", None))
    return jax.shard_map(shards, mesh=mesh, in_specs=in_specs, out_specs=out_specs, check_vma=False)
```

```python
import jax
import jax.numpy as jnp
from jax import lax
from jax.experimental import pallas as pl
from jax.experimental.pallas import tpu as pltpu
from jax.sharding import PartitionSpec as P

MESH = pl.DeviceIdType.MESH
X, Z, CORES, Y = 4, 8, 2, 4
UNITS = 4
NEG = -1e30
F32 = jnp.float32
BF16 = jnp.bfloat16
VMEM_LIMIT = 56 * 1024 * 1024

NT = (((1,), (1,)), ((), ()))
TN = (((0,), (0,)), ((), ()))


def vmem():
    return pl.BlockSpec(memory_space=pltpu.VMEM)


def layer_kernel(
    source_ref, windows_ref, grid_ref, target_ref, count_ref, bias_ref, latent_ref, proj_ref,
    gain_ref, offset_ref, big_hbm, out_hbm, cotangent_hbm,
    processed_ref, gradient_ref, table, stage, outgoing, incoming, rest_out, rest_in, latent_t, proj_t, counts,
    targets, biases, acc, peak_ref, total_ref, send, recv, rest_send, rest_recv,
    big, out_proj, cotangent, fetched, hidden_ref, extended, mixed_rows, offsets, tables,
    attended_t, attended, halo_send, halo_recv, grads, from_core, merged, v_in, v_sum, w_in,
    r_all, core_send, core_recv, y_send, y_recv, w_send, w_recv, r_send, r_recv,
):
    seq = lax.axis_index("seq")
    y = lax.axis_index("dp")
    core = seq % CORES
    z = (seq // CORES) % Z
    x = seq // (CORES * Z)
    channels = grid_ref.shape[1]
    owners, capacity = source_ref.shape
    rows, width = latent_ref.shape
    heads = peak_ref.shape[0]
    size = width // heads
    half = capacity // 2
    group = CORES * UNITS
    main, rest = outgoing.shape[1], rest_out.shape[1]
    depth = main + 16

    def shifts(turn, chip_at):
        pair_at, unit = turn * (UNITS // 2) + chip_at // 2, chip_at % 2
        lap, leg = pair_at // 4, pair_at % 4
        x_shift = 2 + (1 - 2 * (lap % 2)) * ((lap + 1) // 2)
        z_shift = (1 - unit) * (4 - leg) + unit * (leg + 4 * ((leg + 3) // 4))
        return x_shift, z_shift

    barrier = pltpu.get_barrier_semaphore()

    def greet(offset, carry):
        pl.semaphore_signal(
            barrier, inc=1, device_id=(y, (seq + offset) % owners), device_id_type=MESH
        )
        return carry

    lax.fori_loop(1, owners, greet, 0)
    y_peers = [((y + k) % Y, seq) for k in range(1, Y)]
    for peer in y_peers:
        pl.semaphore_signal(barrier, inc=1, device_id=peer, device_id_type=MESH)
    fetches = [
        pltpu.make_async_copy(big_hbm, big, fetched.at[0]),
        pltpu.make_async_copy(out_hbm, out_proj, fetched.at[1]),
        pltpu.make_async_copy(cotangent_hbm, cotangent, fetched.at[2]),
    ]
    for fetch in fetches:
        fetch.start()
    stage[...] = jnp.zeros_like(stage)

    def turn_fields(chunk, carry):
        start = pl.multiple_of(chunk * 128, 128)
        stage[0:channels, :] = grid_ref[0, :, pl.ds(start, 128)].astype(F32)
        table[pl.ds(start, 128), :] = stage[...].T
        return carry

    lax.fori_loop(0, grid_ref.shape[2] // 128, turn_fields, 0)
    pl.semaphore_wait(barrier, owners - 1 + Y - 1)

    def block_copy(step):
        x_shift, z_shift = shifts(step // group, (step // CORES) % UNITS)
        to_x = (x + x_shift) % X
        to_z = (z + z_shift) % Z
        to = to_x * (Z * CORES) + to_z * CORES + step % CORES
        slot = step - step % CORES + core
        copy = pltpu.make_async_remote_copy(
            src_ref=outgoing.at[step], dst_ref=incoming.at[slot],
            send_sem=send.at[step], recv_sem=recv.at[slot],
            device_id=(y, to), device_id_type=MESH,
        )
        rest_copy = pltpu.make_async_remote_copy(
            src_ref=rest_out.at[step], dst_ref=rest_in.at[slot],
            send_sem=rest_send.at[step], recv_sem=rest_recv.at[slot],
            device_id=(y, to), device_id_type=MESH,
        )
        return to, copy, rest_copy

    def send_step(step, carry):
        to, copy, rest_copy = block_copy(step)
        for slot in range(capacity):
            row = (slot % 2) * half + slot // 2
            stage[row : row + 1, :] = table[pl.ds(source_ref[to, slot], 1), :]
        turned = stage[...].T
        block = turned[0:main, :].astype(BF16)
        left = turned[main : main + rest, :]

        @pl.when(to == seq)
        def keep():
            incoming[step] = block
            rest_in[step] = left

        @pl.when(to != seq)
        def pass_on():
            outgoing[step] = block
            rest_out[step] = left
            copy.start()
            rest_copy.start()

        return carry

    lax.fori_loop(0, owners, send_step, 0)

    for chunk in range(width // 128):
        here = slice(chunk * 128, (chunk + 1) * 128)
        latent_t[here, :] = latent_ref[:, here].astype(F32).T.astype(BF16)
    stage[...] = jnp.zeros_like(stage)

    def turn_proj(chunk, carry):
        start = pl.multiple_of(chunk * 128, 128)
        stage[0:channels, :] = proj_ref[:, pl.ds(start, 128)].astype(F32)
        proj_t[pl.ds(start, 128), :] = stage[...].T.astype(BF16)
        return carry

    lax.fori_loop(0, 2 * width // 128, turn_proj, 0)

    chips = owners // CORES
    lane = lax.broadcasted_iota(jnp.int32, (chips, capacity), 1)
    slot_row = lax.broadcasted_iota(jnp.int32, (capacity, capacity), 0)
    slot_lane = lax.broadcasted_iota(jnp.int32, (capacity, capacity), 1)
    owner_lane = lax.broadcasted_iota(jnp.int32, (owners, owners), 1)
    own = jnp.sum(jnp.where(owner_lane == seq, count_ref[...], 0), axis=1, keepdims=True)
    counts[...] = jnp.broadcast_to(own, (owners, capacity))

    def of_core(ref, which):
        return ref[pl.ds(which, chips, stride=CORES), :]

    def picks(parity, which):
        wanted = slot_row == 2 * (slot_lane - which * half) + parity
        in_half = (slot_lane >= which * half) & (slot_lane < (which + 1) * half)
        return jnp.where(wanted & in_half, 1.0, 0.0)

    found = jnp.zeros((chips, capacity), F32)
    for which in range(CORES):
        found = found + jnp.dot(
            of_core(target_ref, which).astype(F32), picks(0, which),
            precision=lax.Precision.HIGHEST, preferred_element_type=F32,
        )
    targets[...] = found.astype(jnp.int32)
    live = jnp.where(lane < half, of_core(counts, 0), of_core(counts, 1))
    for parity in range(2):
        found = jnp.zeros((chips, capacity), F32)
        for which in range(CORES):
            found = found + jnp.dot(
                of_core(bias_ref, which), picks(parity, which),
                precision=lax.Precision.HIGHEST, preferred_element_type=F32,
            )
        biases[parity] = jnp.where(2 * (lane % half) + parity < live, found, NEG)

    span, reach = tables.shape[2], tables.shape[3] // 2
    last = owners - 1

    @pl.when(seq == 0)
    def no_before():
        extended[0:reach, :] = jnp.zeros((reach, width), BF16)

    @pl.when(seq == last)
    def no_after():
        extended[reach + rows :, :] = jnp.zeros((reach, width), BF16)

    offsets[...] = jnp.zeros_like(offsets)
    offsets[:, 0 : 2 * reach + 1] = offset_ref[...]
    key_lane = lax.broadcasted_iota(jnp.int32, (1, span), 1)
    key_row = lax.broadcasted_iota(jnp.int32, (span, reach), 0)
    edges = [
        jnp.where((key_row < reach) & (seq == 0), NEG, 0.0),
        jnp.where((key_row >= 2 * reach) & (seq == last), NEG, 0.0),
    ]

    def table_step(pair, carry):
        for side in range(2):
            head = pair * 2 + side
            row = jnp.where(
                jnp.abs(key_lane - reach) <= windows_ref[head], offsets[pl.ds(head, 1), :], NEG
            )
            row = jnp.broadcast_to(row, (reach, span))
            spread = pltpu.roll(row, 0, 1, stride=1, stride_axis=0).T
            for block in range(2):
                tables[block, pair, :, side * reach : (side + 1) * reach] = spread + edges[block]
        return carry

    lax.fori_loop(0, heads // 2, table_step, 0)

    acc[...] = jnp.zeros_like(acc)
    peak_ref[...] = jnp.zeros_like(peak_ref)
    total_ref[...] = jnp.ones_like(total_ref)
    pairs = UNITS * capacity
    low = lax.broadcasted_iota(jnp.int32, (depth, capacity), 1) < half
    peak_lane = lax.broadcasted_iota(jnp.int32, (rows, 128), 1)
    row_index = lax.broadcasted_iota(jnp.int32, (rows, pairs), 0)

    def group_step(turn, carry):
        for member_at in range(group):
            slot = turn * group + member_at

            @pl.when(slot != 25 * CORES + core)
            def arrive():
                pltpu.make_async_copy(
                    incoming.at[slot], incoming.at[slot], recv.at[slot]
                ).wait()
                pltpu.make_async_copy(
                    rest_in.at[slot], rest_in.at[slot], rest_recv.at[slot]
                ).wait()

        def arrived(slot):
            blank = jnp.zeros((depth - main - rest, capacity), F32)
            return jnp.concatenate([incoming[slot].astype(F32), rest_in[slot], blank], axis=0)

        evens, odds, rows_of, bias_of = [], [], [], [[], []]
        for unit in range(UNITS):
            first = arrived(turn * group + CORES * unit)
            second = arrived(turn * group + CORES * unit + 1)
            evens.append(jnp.where(low, first, pltpu.roll(second, half, 1)).astype(BF16))
            odds.append(jnp.where(low, pltpu.roll(first, half, 1), second).astype(BF16))
            x_shift, z_shift = shifts(turn, unit)
            chip = ((x + X - x_shift) % X) * Z + (z + Z - z_shift) % Z
            rows_of.append(targets[pl.ds(chip, 1), :])
            for parity in range(2):
                bias_of[parity].append(biases[parity, pl.ds(chip, 1), :])
        target = jnp.concatenate(rows_of, axis=1)
        member = row_index == target
        chosen = jnp.where(member, 1.0, 0.0).astype(BF16)
        queries = jnp.dot(latent_t[...], chosen, preferred_element_type=F32)
        scores, fields = [], []
        for parity, parts in enumerate((evens, odds)):
            part = jnp.concatenate(parts, axis=1)
            keys = jnp.dot(proj_t[0:width, 0:depth], part, preferred_element_type=F32)
            logits = jnp.sum((queries * keys).reshape(heads, size, pairs), axis=1)
            scores.append(logits * (size ** -0.5) + jnp.concatenate(bias_of[parity], axis=1))
            fields.append(part)
        pair_peak = jnp.maximum(scores[0], scores[1])
        peaks = jnp.full((rows, 128), NEG, F32)
        for head in range(heads):
            column = jnp.max(
                jnp.where(member, pair_peak[head : head + 1, :], NEG), axis=1, keepdims=True
            )
            peaks = jnp.where(peak_lane == head, column, peaks)
        old = peak_ref[...]
        new = jnp.maximum(old, peaks.T[0:heads, :])
        upper = new.astype(BF16)
        lower = (new - upper.astype(F32)).astype(BF16)
        new = upper.astype(F32) + lower.astype(F32)
        peak_ref[...] = new
        factor = jnp.exp(old - new)
        slot_peak = jnp.dot(upper, chosen, preferred_element_type=F32) + jnp.dot(
            lower, chosen, preferred_element_type=F32
        )
        weights = [jnp.exp(score - slot_peak) for score in scores]
        both = weights[0] + weights[1]
        both_upper = both.astype(BF16)
        both_lower = (both - both_upper.astype(F32)).astype(BF16)
        sums = lax.dot_general(both_upper, chosen, NT, preferred_element_type=F32)
        sums = sums + lax.dot_general(both_lower, chosen, NT, preferred_element_type=F32)
        total_ref[...] = total_ref[...] * factor + sums
        mixed = None
        for parity in range(2):
            values = jnp.dot(
                proj_t[width : 2 * width, 0:depth], fields[parity], preferred_element_type=F32
            )
            term = values.reshape(heads, size, pairs) * weights[parity][:, None, :]
            mixed = term if mixed is None else mixed + term
        mixed = mixed.reshape(width, pairs).astype(BF16)
        added = lax.dot_general(mixed, chosen, NT, preferred_element_type=F32)
        acc[...] = (
            acc[...].reshape(heads, size, rows) * factor[:, None, :]
        ).reshape(width, rows) + added
        return carry

    lax.fori_loop(0, owners // group, group_step, 0)

    scale = 1.0 / total_ref[...]
    encoded = (acc[...].reshape(heads, size, rows) * scale[:, None, :]).reshape(width, rows)
    hidden = latent_ref[...].astype(F32) + encoded.T
    hidden_ref[...] = hidden
    center = hidden - jnp.mean(hidden, axis=1, keepdims=True)
    variance = jnp.mean(center * center, axis=1, keepdims=True)
    extended[reach : reach + rows, :] = (
        center * lax.rsqrt(variance + 1e-05) * gain_ref[...]
    ).astype(BF16)

    def halo_copy(which, there, here, to):
        return pltpu.make_async_remote_copy(
            src_ref=extended.at[there], dst_ref=extended.at[here],
            send_sem=halo_send.at[which], recv_sem=halo_recv.at[which],
            device_id=(y, to), device_id_type=MESH,
        )

    up = halo_copy(0, pl.ds(rows, reach), pl.ds(0, reach), (seq + 1) % owners)
    down = halo_copy(
        1, pl.ds(reach, reach), pl.ds(reach + rows, reach), (seq + owners - 1) % owners
    )
    pl.when(seq < last)(up.start)
    pl.when(seq > 0)(down.start)

    tile = 512
    for fetch in fetches:
        fetch.wait()

    def own_tile(index, carry):
        at = pl.ds(pl.multiple_of(index * tile, tile), tile)
        found = jnp.dot(
            extended[reach : reach + rows, :], big[:, at], preferred_element_type=F32
        )
        scaling = jnp.where(index * tile < width, size ** -0.5, 1.0)
        mixed_rows[reach : reach + rows, at] = (found * scaling).astype(BF16)
        return carry

    lax.fori_loop(0, 3 * width // tile, own_tile, 0)
    pl.when(seq > 0)(up.wait_recv)
    pl.when(seq < last)(down.wait_recv)

    def halo_tile(index, carry):
        at = pl.ds(pl.multiple_of(index * tile + width, tile), tile)
        both = jnp.concatenate([extended[0:reach, :], extended[reach + rows :, :]], axis=0)
        found = jnp.dot(both, big[:, at], preferred_element_type=F32).astype(BF16)
        mixed_rows[0:reach, at] = found[0:reach]
        mixed_rows[reach + rows :, at] = found[reach:]
        return carry

    lax.fori_loop(0, 2 * width // tile, halo_tile, 0)

    def place(y_to, x_to, z_to, core_to):
        return (y_to, x_to * (Z * CORES) + z_to * CORES + core_to)

    def remote(src_ref, dst_ref, send_sem, recv_sem, peer):
        return pltpu.make_async_remote_copy(
            src_ref=src_ref, dst_ref=dst_ref, send_sem=send_sem, recv_sem=recv_sem,
            device_id=peer, device_id_type=MESH,
        )

    part_width = width // X
    strip_width = width // Y

    def strip(who):
        return pl.ds(pl.multiple_of(who * strip_width, strip_width), strip_width)

    def part_of(turn):
        return (x + 1 + turn) % X

    def core_copy(turn):
        part = part_of(turn)
        return remote(
            grads.at[part, :, 1 - core], from_core.at[part], core_send.at[part],
            core_recv.at[part], place(y, x, z, 1 - core),
        )

    def y_copy(turn, k):
        part = part_of(turn)
        return remote(
            merged.at[part, :, :, strip((y + k) % Y)], v_in.at[k - 1, part],
            y_send.at[k - 1, part], y_recv.at[k - 1, part], y_peers[k - 1],
        )

    def w_copy(turn, k):
        part = part_of(turn)
        to_z = (z + k) % Z
        return remote(
            v_sum.at[part, to_z], w_in.at[turn, k], w_send.at[turn, k], w_recv.at[turn, k],
            place(y, part, to_z, core),
        )

    def pass_to_y(turn):
        part = part_of(turn)
        core_copy(turn).wait_recv()
        merged[part] = (
            grads[part, :, core].astype(F32) + from_core[part].astype(F32)
        ).astype(BF16)
        for k in range(1, Y):
            y_copy(turn, k).start()

    def pass_to_owners(turn, first):
        part = part_of(turn)
        for k in range(1, Y):
            y_copy(turn, k).wait_recv()
        v_sum[part] = (
            merged[part, :, :, strip(y)].astype(F32)
            + (v_in[0, part].astype(F32) + v_in[1, part].astype(F32) + v_in[2, part].astype(F32))
        ).astype(BF16)
        for k in range(first, Z):
            w_copy(turn, k).start()

    side_lane = lax.broadcasted_iota(jnp.int32, (reach, 2 * size), 1) < size

    def part_step(turn, carry):
        part = part_of(turn)

        def columns(base, pair):
            at = base + part * part_width + pair * 2 * size
            return pl.ds(pl.multiple_of(at, 2 * size), 2 * size)

        pairs_in_part = part_width // (2 * size)
        for block in range(2):
            if block == 1:
                pl.when(turn > 0)(lambda: pass_to_y(turn - 1))
            mine = slice((block + 1) * reach, (block + 2) * reach)
            theirs = slice(block * reach, block * reach + span)
            for pair in range(pairs_in_part):
                queries = mixed_rows[mine, columns(0, pair)]
                none = jnp.zeros_like(queries)
                queries = jnp.concatenate(
                    [jnp.where(side_lane, queries, none), jnp.where(side_lane, none, queries)],
                    axis=0,
                )
                logits = lax.dot_general(
                    mixed_rows[theirs, columns(width, pair)], queries, NT,
                    preferred_element_type=F32,
                ) + tables[block, part * pairs_in_part + pair]
                powered = jnp.exp(logits - jnp.max(logits, axis=0, keepdims=True))
                scale = 1.0 / jnp.sum(powered, axis=0, keepdims=True)
                mixture = lax.dot_general(
                    mixed_rows[theirs, columns(2 * width, pair)], powered.astype(BF16), TN,
                    preferred_element_type=F32,
                ) * scale
                across = slice(block * reach, (block + 1) * reach)
                for side in range(2):
                    down_at = part * part_width + (pair * 2 + side) * size
                    attended_t[pl.ds(pl.multiple_of(down_at, size), size), across] = mixture[
                        side * size : (side + 1) * size, side * reach : (side + 1) * reach
                    ].astype(BF16)
        found = jnp.dot(
            attended_t[pl.ds(pl.multiple_of(part * part_width, part_width), part_width), :],
            cotangent[0], preferred_element_type=F32,
        )
        grads[part] = found.astype(BF16).reshape(Z, CORES, 16, width)
        core_copy(turn).start()
        return carry

    lax.fori_loop(0, X, part_step, 0)
    pass_to_owners(0, 0)
    attended[...] = attended_t[...].astype(F32).T.astype(BF16)

    def out_tile(index):
        at = slice(index * tile, (index + 1) * tile)
        processed_ref[:, at] = (
            hidden_ref[:, at]
            + jnp.dot(attended[...], out_proj[:, at], preferred_element_type=F32)
        ).astype(BF16)

    pass_to_y(X - 1)
    for turn in range(1, X - 1):
        pass_to_owners(turn, 0)
        out_tile(turn - 1)
    pass_to_owners(X - 1, 1)
    total = v_sum[x, z].astype(F32)
    for turn in range(X):
        for k in range(1 if turn == X - 1 else 0, Z):
            w_copy(turn, k).wait_recv()
            total = total + w_in[turn, k].astype(F32)
    r_all[y] = total
    r_copies = [
        remote(r_all.at[y], r_all.at[y], r_send.at[k - 1], r_recv.at[k - 1], y_peers[k - 1])
        for k in range(1, Y)
    ]
    for copy in r_copies:
        copy.start()

    def sent_step(step, carry):
        to, copy, rest_copy = block_copy(step)

        @pl.when(to != seq)
        def done():
            copy.wait_send()
            rest_copy.wait_send()

        return carry

    lax.fori_loop(0, owners, sent_step, 0)
    pl.when(seq < last)(up.wait_send)
    pl.when(seq > 0)(down.wait_send)
    for turn in range(X):
        core_copy(turn).wait_send()
        for k in range(1, Y):
            y_copy(turn, k).wait_send()
        for k in range(1 if turn == X - 1 else 0, Z):
            w_copy(turn, k).wait_send()
    for copy in r_copies:
        copy.wait_recv()
    for k in range(Y):
        gradient_ref[:, k * strip_width : (k + 1) * strip_width] = r_all[k]
    for copy in r_copies:
        copy.wait_send()


def place_kernel(processed_ref, gradient_ref, processed_out, gradient_out):
    processed_out[0] = processed_ref[...]
    gradient_out[...] = gradient_ref[...]


def shards(
    grid_fields, mesh_latent, edge_source, edge_target, edge_count, edge_bias, encoder_proj,
    norm_gain, processor_proj, offset_bias, windows, output_proj, cotangent,
):
    shard_count = lax.axis_size("seq")
    device = lax.axis_index("seq")
    rows, width = mesh_latent.shape
    heads = offset_bias.shape[0]
    reach = (offset_bias.shape[1] - 1) // 2
    channels, points = grid_fields.shape[1:]
    capacity = edge_source.shape[2]
    main = channels // 16 * 16
    chips = shard_count // CORES
    strip_width = width // Y
    dma = pltpu.SemaphoreType.DMA
    hbm = pl.BlockSpec(memory_space=pltpu.HBM)
    processed, gradient = pl.pallas_call(
        layer_kernel,
        out_shape=(
            jax.ShapeDtypeStruct((rows, width), BF16),
            jax.ShapeDtypeStruct((16, width), F32),
        ),
        in_specs=[pl.BlockSpec(memory_space=pltpu.SMEM)] * 2 + [vmem()] * 8 + [hbm] * 3,
        out_specs=(vmem(), vmem()),
        scratch_shapes=[
            pltpu.VMEM((points, 128), F32),
            pltpu.VMEM((128, 128), F32),
            pltpu.VMEM((shard_count, main, capacity), BF16),
            pltpu.VMEM((shard_count, main, capacity), BF16),
            pltpu.VMEM((shard_count, channels - main, capacity), F32),
            pltpu.VMEM((shard_count, channels - main, capacity), F32),
            pltpu.VMEM((width, rows), BF16),
            pltpu.VMEM((2 * width, 128), BF16),
            pltpu.VMEM((shard_count, capacity), jnp.int32),
            pltpu.VMEM((chips, capacity), jnp.int32),
            pltpu.VMEM((2, chips, capacity), F32),
            pltpu.VMEM((width, rows), F32),
            pltpu.VMEM((heads, rows), F32),
            pltpu.VMEM((heads, rows), F32),
            dma((shard_count,)),
            dma((shard_count,)),
            dma((shard_count,)),
            dma((shard_count,)),
            pltpu.VMEM((width, 3 * width), BF16),
            pltpu.VMEM((width, width), BF16),
            pltpu.VMEM((1, rows, width), BF16),
            dma((3,)),
            pltpu.VMEM((rows, width), F32),
            pltpu.VMEM((rows + 2 * reach, width), BF16),
            pltpu.VMEM((rows + 2 * reach, 3 * width), BF16),
            pltpu.VMEM((heads, 3 * reach), F32),
            pltpu.VMEM((2, heads // 2, 3 * reach, 2 * reach), F32),
            pltpu.VMEM((width, rows), BF16),
            pltpu.VMEM((rows, width), BF16),
            dma((2,)),
            dma((2,)),
            pltpu.VMEM((X, Z, CORES, 16, width), BF16),
            pltpu.VMEM((X, Z, 16, width), BF16),
            pltpu.VMEM((X, Z, 16, width), BF16),
            pltpu.VMEM((Y - 1, X, Z, 16, strip_width), BF16),
            pltpu.VMEM((X, Z, 16, strip_width), BF16),
            pltpu.VMEM((X, Z, 16, strip_width), BF16),
            pltpu.VMEM((Y, 16, strip_width), F32),
            dma((X,)),
            dma((X,)),
            dma((Y - 1, X)),
            dma((Y - 1, X)),
            dma((X, Z)),
            dma((X, Z)),
            dma((Y - 1,)),
            dma((Y - 1,)),
        ],
        compiler_params=pltpu.CompilerParams(
            vmem_limit_bytes=VMEM_LIMIT, collective_id=2, has_side_effects=True
        ),
        name="layer",
    )(
        edge_source[0], windows, grid_fields, edge_target[0], edge_count, edge_bias[0], mesh_latent,
        encoder_proj, norm_gain[None], offset_bias, processor_proj, output_proj, cotangent,
    )

    return pl.pallas_call(
        place_kernel,
        out_shape=(
            jax.ShapeDtypeStruct((1, rows, width), BF16),
            jax.ShapeDtypeStruct((16, width), F32),
        ),
        in_specs=[vmem(), vmem()],
        out_specs=(vmem(), vmem()),
        name="place",
    )(processed, gradient)


def solution(mesh):
    in_specs = (
        P("dp", None, "seq"),
        P("seq", None),
        P("seq", None, None),
        P("seq", None, None),
        P(),
        P("seq", None, None),
        P(),
        P(),
        P(),
        P(),
        P(),
        P(),
        P("dp", "seq", None),
    )
    out_specs = (P("dp", "seq", None), P("seq", None))
    return jax.shard_map(shards, mesh=mesh, in_specs=in_specs, out_specs=out_specs, check_vma=False)
```

```python
import jax
import jax.numpy as jnp
from jax import lax
from jax.experimental import pallas as pl
from jax.experimental.pallas import tpu as pltpu
from jax.sharding import PartitionSpec as P

MESH = pl.DeviceIdType.MESH
X, Z, CORES, Y = 4, 8, 2, 4
UNITS = 4
NEG = -1e30
F32 = jnp.float32
BF16 = jnp.bfloat16
VMEM_LIMIT = 56 * 1024 * 1024

NT = (((1,), (1,)), ((), ()))
TN = (((0,), (0,)), ((), ()))


def vmem():
    return pl.BlockSpec(memory_space=pltpu.VMEM)


def layer_kernel(
    source_ref, windows_ref, grid_ref, target_ref, count_ref, bias_ref, latent_ref, proj_ref,
    gain_ref, offset_ref, big_hbm, out_hbm, cotangent_hbm,
    processed_ref, gradient_ref, table, stage, outgoing, incoming, rest_out, rest_in, latent_t, proj_t, counts,
    targets, biases, acc, peak_ref, total_ref, send, recv, rest_send, rest_recv,
    big, out_proj, cotangent, fetched, hidden_ref, extended, mixed_rows, offsets, tables,
    attended_t, attended, halo_send, halo_recv, grads, from_core, merged, v_in, v_sum, w_in,
    r_all, x_in, x_sum, z_in, y_all, core_send, core_recv, y_send, y_recv, w_send, w_recv,
    r_send, r_recv, x_send, x_recv, z_send, z_recv, s_send, s_recv,
):
    seq = lax.axis_index("seq")
    y = lax.axis_index("dp")
    core = seq % CORES
    z = (seq // CORES) % Z
    x = seq // (CORES * Z)
    channels = grid_ref.shape[1]
    owners, capacity = source_ref.shape
    rows, width = latent_ref.shape
    heads = peak_ref.shape[0]
    size = width // heads
    half = capacity // 2
    group = CORES * UNITS
    main, rest = outgoing.shape[1], rest_out.shape[1]
    depth = main + 16

    def shifts(turn, chip_at):
        pair_at, unit = turn * (UNITS // 2) + chip_at // 2, chip_at % 2
        lap, leg = pair_at // 4, pair_at % 4
        x_shift = 2 + (1 - 2 * (lap % 2)) * ((lap + 1) // 2)
        z_shift = (1 - unit) * (4 - leg) + unit * (leg + 4 * ((leg + 3) // 4))
        return x_shift, z_shift

    barrier = pltpu.get_barrier_semaphore()

    def greet(offset, carry):
        pl.semaphore_signal(
            barrier, inc=1, device_id=(y, (seq + offset) % owners), device_id_type=MESH
        )
        return carry

    lax.fori_loop(1, owners, greet, 0)
    y_peers = [((y + k) % Y, seq) for k in range(1, Y)]
    for peer in y_peers:
        pl.semaphore_signal(barrier, inc=1, device_id=peer, device_id_type=MESH)
    fetches = [
        pltpu.make_async_copy(big_hbm, big, fetched.at[0]),
        pltpu.make_async_copy(out_hbm, out_proj, fetched.at[1]),
        pltpu.make_async_copy(cotangent_hbm, cotangent, fetched.at[2]),
    ]
    for fetch in fetches:
        fetch.start()
    stage[...] = jnp.zeros_like(stage)

    def turn_fields(chunk, carry):
        start = pl.multiple_of(chunk * 128, 128)
        stage[0:channels, :] = grid_ref[0, :, pl.ds(start, 128)].astype(F32)
        table[pl.ds(start, 128), :] = stage[...].T
        return carry

    lax.fori_loop(0, grid_ref.shape[2] // 128, turn_fields, 0)
    pl.semaphore_wait(barrier, owners - 1 + Y - 1)

    def block_copy(step):
        x_shift, z_shift = shifts(step // group, (step // CORES) % UNITS)
        to_x = (x + x_shift) % X
        to_z = (z + z_shift) % Z
        to = to_x * (Z * CORES) + to_z * CORES + step % CORES
        slot = step - step % CORES + core
        copy = pltpu.make_async_remote_copy(
            src_ref=outgoing.at[step], dst_ref=incoming.at[slot],
            send_sem=send.at[step], recv_sem=recv.at[slot],
            device_id=(y, to), device_id_type=MESH,
        )
        rest_copy = pltpu.make_async_remote_copy(
            src_ref=rest_out.at[step], dst_ref=rest_in.at[slot],
            send_sem=rest_send.at[step], recv_sem=rest_recv.at[slot],
            device_id=(y, to), device_id_type=MESH,
        )
        return to, copy, rest_copy

    def send_step(step, carry):
        to, copy, rest_copy = block_copy(step)
        for slot in range(capacity):
            row = (slot % 2) * half + slot // 2
            stage[row : row + 1, :] = table[pl.ds(source_ref[to, slot], 1), :]
        turned = stage[...].T
        block = turned[0:main, :].astype(BF16)
        left = turned[main : main + rest, :]

        @pl.when(to == seq)
        def keep():
            incoming[step] = block
            rest_in[step] = left

        @pl.when(to != seq)
        def pass_on():
            outgoing[step] = block
            rest_out[step] = left
            copy.start()
            rest_copy.start()

        return carry

    lax.fori_loop(0, owners, send_step, 0)

    for chunk in range(width // 128):
        here = slice(chunk * 128, (chunk + 1) * 128)
        latent_t[here, :] = latent_ref[:, here].astype(F32).T.astype(BF16)
    stage[...] = jnp.zeros_like(stage)

    def turn_proj(chunk, carry):
        start = pl.multiple_of(chunk * 128, 128)
        stage[0:channels, :] = proj_ref[:, pl.ds(start, 128)].astype(F32)
        proj_t[pl.ds(start, 128), :] = stage[...].T.astype(BF16)
        return carry

    lax.fori_loop(0, 2 * width // 128, turn_proj, 0)

    chips = owners // CORES
    lane = lax.broadcasted_iota(jnp.int32, (chips, capacity), 1)
    slot_row = lax.broadcasted_iota(jnp.int32, (capacity, capacity), 0)
    slot_lane = lax.broadcasted_iota(jnp.int32, (capacity, capacity), 1)
    owner_lane = lax.broadcasted_iota(jnp.int32, (owners, owners), 1)
    own = jnp.sum(jnp.where(owner_lane == seq, count_ref[...], 0), axis=1, keepdims=True)
    counts[...] = jnp.broadcast_to(own, (owners, capacity))

    def of_core(ref, which):
        return ref[pl.ds(which, chips, stride=CORES), :]

    def picks(parity, which):
        wanted = slot_row == 2 * (slot_lane - which * half) + parity
        in_half = (slot_lane >= which * half) & (slot_lane < (which + 1) * half)
        return jnp.where(wanted & in_half, 1.0, 0.0)

    found = jnp.zeros((chips, capacity), F32)
    for which in range(CORES):
        found = found + jnp.dot(
            of_core(target_ref, which).astype(F32), picks(0, which),
            precision=lax.Precision.HIGHEST, preferred_element_type=F32,
        )
    targets[...] = found.astype(jnp.int32)
    live = jnp.where(lane < half, of_core(counts, 0), of_core(counts, 1))
    for parity in range(2):
        found = jnp.zeros((chips, capacity), F32)
        for which in range(CORES):
            found = found + jnp.dot(
                of_core(bias_ref, which), picks(parity, which),
                precision=lax.Precision.HIGHEST, preferred_element_type=F32,
            )
        biases[parity] = jnp.where(2 * (lane % half) + parity < live, found, NEG)

    span, reach = tables.shape[2], tables.shape[3] // 2
    last = owners - 1

    @pl.when(seq == 0)
    def no_before():
        extended[0:reach, :] = jnp.zeros((reach, width), BF16)

    @pl.when(seq == last)
    def no_after():
        extended[reach + rows :, :] = jnp.zeros((reach, width), BF16)

    offsets[...] = jnp.zeros_like(offsets)
    offsets[:, 0 : 2 * reach + 1] = offset_ref[...]
    key_lane = lax.broadcasted_iota(jnp.int32, (1, span), 1)
    key_row = lax.broadcasted_iota(jnp.int32, (span, reach), 0)
    edges = [
        jnp.where((key_row < reach) & (seq == 0), NEG, 0.0),
        jnp.where((key_row >= 2 * reach) & (seq == last), NEG, 0.0),
    ]

    def table_step(pair, carry):
        for side in range(2):
            head = pair * 2 + side
            row = jnp.where(
                jnp.abs(key_lane - reach) <= windows_ref[head], offsets[pl.ds(head, 1), :], NEG
            )
            row = jnp.broadcast_to(row, (reach, span))
            spread = pltpu.roll(row, 0, 1, stride=1, stride_axis=0).T
            for block in range(2):
                tables[block, pair, :, side * reach : (side + 1) * reach] = spread + edges[block]
        return carry

    lax.fori_loop(0, heads // 2, table_step, 0)

    acc[...] = jnp.zeros_like(acc)
    peak_ref[...] = jnp.zeros_like(peak_ref)
    total_ref[...] = jnp.ones_like(total_ref)
    pairs = UNITS * capacity
    low = lax.broadcasted_iota(jnp.int32, (depth, capacity), 1) < half
    peak_lane = lax.broadcasted_iota(jnp.int32, (rows, 128), 1)
    row_index = lax.broadcasted_iota(jnp.int32, (rows, pairs), 0)

    def group_step(turn, carry):
        for member_at in range(group):
            slot = turn * group + member_at

            @pl.when(slot != 25 * CORES + core)
            def arrive():
                pltpu.make_async_copy(
                    incoming.at[slot], incoming.at[slot], recv.at[slot]
                ).wait()
                pltpu.make_async_copy(
                    rest_in.at[slot], rest_in.at[slot], rest_recv.at[slot]
                ).wait()

        def arrived(slot):
            blank = jnp.zeros((depth - main - rest, capacity), F32)
            return jnp.concatenate([incoming[slot].astype(F32), rest_in[slot], blank], axis=0)

        evens, odds, rows_of, bias_of = [], [], [], [[], []]
        for unit in range(UNITS):
            first = arrived(turn * group + CORES * unit)
            second = arrived(turn * group + CORES * unit + 1)
            evens.append(jnp.where(low, first, pltpu.roll(second, half, 1)).astype(BF16))
            odds.append(jnp.where(low, pltpu.roll(first, half, 1), second).astype(BF16))
            x_shift, z_shift = shifts(turn, unit)
            chip = ((x + X - x_shift) % X) * Z + (z + Z - z_shift) % Z
            rows_of.append(targets[pl.ds(chip, 1), :])
            for parity in range(2):
                bias_of[parity].append(biases[parity, pl.ds(chip, 1), :])
        target = jnp.concatenate(rows_of, axis=1)
        member = row_index == target
        chosen = jnp.where(member, 1.0, 0.0).astype(BF16)
        queries = jnp.dot(latent_t[...], chosen, preferred_element_type=F32)
        scores, fields = [], []
        for parity, parts in enumerate((evens, odds)):
            part = jnp.concatenate(parts, axis=1)
            keys = jnp.dot(proj_t[0:width, 0:depth], part, preferred_element_type=F32)
            logits = jnp.sum((queries * keys).reshape(heads, size, pairs), axis=1)
            scores.append(logits * (size ** -0.5) + jnp.concatenate(bias_of[parity], axis=1))
            fields.append(part)
        pair_peak = jnp.maximum(scores[0], scores[1])
        peaks = jnp.full((rows, 128), NEG, F32)
        for head in range(heads):
            column = jnp.max(
                jnp.where(member, pair_peak[head : head + 1, :], NEG), axis=1, keepdims=True
            )
            peaks = jnp.where(peak_lane == head, column, peaks)
        old = peak_ref[...]
        new = jnp.maximum(old, peaks.T[0:heads, :])
        upper = new.astype(BF16)
        lower = (new - upper.astype(F32)).astype(BF16)
        new = upper.astype(F32) + lower.astype(F32)
        peak_ref[...] = new
        factor = jnp.exp(old - new)
        slot_peak = jnp.dot(upper, chosen, preferred_element_type=F32) + jnp.dot(
            lower, chosen, preferred_element_type=F32
        )
        weights = [jnp.exp(score - slot_peak) for score in scores]
        both = weights[0] + weights[1]
        both_upper = both.astype(BF16)
        both_lower = (both - both_upper.astype(F32)).astype(BF16)
        sums = lax.dot_general(both_upper, chosen, NT, preferred_element_type=F32)
        sums = sums + lax.dot_general(both_lower, chosen, NT, preferred_element_type=F32)
        total_ref[...] = total_ref[...] * factor + sums
        mixed = None
        for parity in range(2):
            values = jnp.dot(
                proj_t[width : 2 * width, 0:depth], fields[parity], preferred_element_type=F32
            )
            term = values.reshape(heads, size, pairs) * weights[parity][:, None, :]
            mixed = term if mixed is None else mixed + term
        mixed = mixed.reshape(width, pairs).astype(BF16)
        added = lax.dot_general(mixed, chosen, NT, preferred_element_type=F32)
        acc[...] = (
            acc[...].reshape(heads, size, rows) * factor[:, None, :]
        ).reshape(width, rows) + added
        return carry

    lax.fori_loop(0, owners // group, group_step, 0)

    scale = 1.0 / total_ref[...]
    encoded = (acc[...].reshape(heads, size, rows) * scale[:, None, :]).reshape(width, rows)
    hidden = latent_ref[...].astype(F32) + encoded.T
    hidden_ref[...] = hidden
    center = hidden - jnp.mean(hidden, axis=1, keepdims=True)
    variance = jnp.mean(center * center, axis=1, keepdims=True)
    extended[reach : reach + rows, :] = (
        center * lax.rsqrt(variance + 1e-05) * gain_ref[...]
    ).astype(BF16)

    def halo_copy(which, there, here, to):
        return pltpu.make_async_remote_copy(
            src_ref=extended.at[there], dst_ref=extended.at[here],
            send_sem=halo_send.at[which], recv_sem=halo_recv.at[which],
            device_id=(y, to), device_id_type=MESH,
        )

    up = halo_copy(0, pl.ds(rows, reach), pl.ds(0, reach), (seq + 1) % owners)
    down = halo_copy(
        1, pl.ds(reach, reach), pl.ds(reach + rows, reach), (seq + owners - 1) % owners
    )
    pl.when(seq < last)(up.start)
    pl.when(seq > 0)(down.start)

    tile = 512
    for fetch in fetches:
        fetch.wait()

    def own_tile(index, carry):
        at = pl.ds(pl.multiple_of(index * tile, tile), tile)
        found = jnp.dot(
            extended[reach : reach + rows, :], big[:, at], preferred_element_type=F32
        )
        scaling = jnp.where(index * tile < width, size ** -0.5, 1.0)
        mixed_rows[reach : reach + rows, at] = (found * scaling).astype(BF16)
        return carry

    lax.fori_loop(0, 3 * width // tile, own_tile, 0)
    pl.when(seq > 0)(up.wait_recv)
    pl.when(seq < last)(down.wait_recv)

    def halo_tile(index, carry):
        at = pl.ds(pl.multiple_of(index * tile + width, tile), tile)
        both = jnp.concatenate([extended[0:reach, :], extended[reach + rows :, :]], axis=0)
        found = jnp.dot(both, big[:, at], preferred_element_type=F32).astype(BF16)
        mixed_rows[0:reach, at] = found[0:reach]
        mixed_rows[reach + rows :, at] = found[reach:]
        return carry

    lax.fori_loop(0, 2 * width // tile, halo_tile, 0)

    def place(y_to, x_to, z_to, core_to):
        return (y_to, x_to * (Z * CORES) + z_to * CORES + core_to)

    def remote(src_ref, dst_ref, send_sem, recv_sem, peer):
        return pltpu.make_async_remote_copy(
            src_ref=src_ref, dst_ref=dst_ref, send_sem=send_sem, recv_sem=recv_sem,
            device_id=peer, device_id_type=MESH,
        )

    part_width = width // X
    half_width = width // 2
    strip_width = half_width // Y

    def strip(who):
        return pl.ds(pl.multiple_of(half_width + who * strip_width, strip_width), strip_width)

    def part_of(turn):
        return (x + 1 + turn) % X

    def core_copy(turn):
        part = part_of(turn)
        return remote(
            grads.at[part, :, 1 - core], from_core.at[part], core_send.at[part],
            core_recv.at[part], place(y, x, z, 1 - core),
        )

    def y_copy(turn, k):
        part = part_of(turn)
        return remote(
            merged.at[part, :, :, strip((y + k) % Y)], v_in.at[k - 1, part],
            y_send.at[k - 1, part], y_recv.at[k - 1, part], y_peers[k - 1],
        )

    def x_copy(turn):
        part = part_of(turn)
        return remote(
            merged.at[part, :, :, pl.ds(0, half_width)], x_in.at[turn], x_send.at[turn],
            x_recv.at[turn], place(y, part, z, core),
        )

    def w_copy(turn, k):
        part = part_of(turn)
        to_z = (z + k) % Z
        return remote(
            v_sum.at[part, to_z], w_in.at[turn, k], w_send.at[turn, k], w_recv.at[turn, k],
            place(y, part, to_z, core),
        )

    def pass_to_y(turn, with_x):
        part = part_of(turn)
        core_copy(turn).wait_recv()
        merged[part] = (
            grads[part, :, core].astype(F32) + from_core[part].astype(F32)
        ).astype(BF16)
        if with_x:
            x_copy(turn).start()
        for k in range(1, Y):
            y_copy(turn, k).start()

    def pass_to_owners(turn, first):
        part = part_of(turn)
        for k in range(1, Y):
            y_copy(turn, k).wait_recv()
        v_sum[part] = (
            merged[part, :, :, strip(y)].astype(F32)
            + (v_in[0, part].astype(F32) + v_in[1, part].astype(F32) + v_in[2, part].astype(F32))
        ).astype(BF16)
        for k in range(first, Z):
            w_copy(turn, k).start()

    side_lane = lax.broadcasted_iota(jnp.int32, (reach, 2 * size), 1) < size

    def part_step(turn, carry):
        part = part_of(turn)

        def columns(base, pair):
            at = base + part * part_width + pair * 2 * size
            return pl.ds(pl.multiple_of(at, 2 * size), 2 * size)

        pairs_in_part = part_width // (2 * size)
        for block in range(2):
            if block == 1:
                pl.when(turn > 0)(lambda: pass_to_y(turn - 1, True))
            mine = slice((block + 1) * reach, (block + 2) * reach)
            theirs = slice(block * reach, block * reach + span)
            for pair in range(pairs_in_part):
                queries = mixed_rows[mine, columns(0, pair)]
                none = jnp.zeros_like(queries)
                queries = jnp.concatenate(
                    [jnp.where(side_lane, queries, none), jnp.where(side_lane, none, queries)],
                    axis=0,
                )
                logits = lax.dot_general(
                    mixed_rows[theirs, columns(width, pair)], queries, NT,
                    preferred_element_type=F32,
                ) + tables[block, part * pairs_in_part + pair]
                powered = jnp.exp(logits - jnp.max(logits, axis=0, keepdims=True))
                scale = 1.0 / jnp.sum(powered, axis=0, keepdims=True)
                mixture = lax.dot_general(
                    mixed_rows[theirs, columns(2 * width, pair)], powered.astype(BF16), TN,
                    preferred_element_type=F32,
                ) * scale
                across = slice(block * reach, (block + 1) * reach)
                for side in range(2):
                    down_at = part * part_width + (pair * 2 + side) * size
                    attended_t[pl.ds(pl.multiple_of(down_at, size), size), across] = mixture[
                        side * size : (side + 1) * size, side * reach : (side + 1) * reach
                    ].astype(BF16)
        found = jnp.dot(
            attended_t[pl.ds(pl.multiple_of(part * part_width, part_width), part_width), :],
            cotangent[0], preferred_element_type=F32,
        )
        grads[part] = found.astype(BF16).reshape(Z, CORES, 16, width)
        core_copy(turn).start()
        return carry

    lax.fori_loop(0, X, part_step, 0)
    pass_to_owners(0, 0)
    attended[...] = attended_t[...].astype(F32).T.astype(BF16)

    def out_tile(index):
        at = slice(index * tile, (index + 1) * tile)
        processed_ref[:, at] = (
            hidden_ref[:, at]
            + jnp.dot(attended[...], out_proj[:, at], preferred_element_type=F32)
        ).astype(BF16)

    pass_to_y(X - 1, False)
    pass_to_owners(1, 0)
    out_tile(0)
    part = merged[x, :, :, 0:half_width].astype(F32)
    for turn in range(X - 1):
        x_copy(turn).wait_recv()
        part = part + x_in[turn].astype(F32)
    x_sum[...] = part.astype(BF16)
    z_copies = [
        remote(
            x_sum.at[(z + k) % Z], z_in.at[k - 1], z_send.at[k - 1], z_recv.at[k - 1],
            place(y, x, (z + k) % Z, core),
        )
        for k in range(1, Z)
    ]
    for copy in z_copies:
        copy.start()
    pass_to_owners(2, 0)
    out_tile(1)
    pass_to_owners(X - 1, 1)

    def to_dp(ref, send_sem, recv_sem):
        copies = [
            remote(ref.at[y], ref.at[y], send_sem.at[k - 1], recv_sem.at[k - 1], y_peers[k - 1])
            for k in range(1, Y)
        ]
        for copy in copies:
            copy.start()
        return copies

    total = x_sum[z].astype(F32)
    for k in range(1, Z):
        z_copies[k - 1].wait_recv()
        total = total + z_in[k - 1].astype(F32)
    y_all[y] = total
    s_copies = to_dp(y_all, s_send, s_recv)
    total = v_sum[x, z].astype(F32)
    for turn in range(X):
        for k in range(1 if turn == X - 1 else 0, Z):
            w_copy(turn, k).wait_recv()
            total = total + w_in[turn, k].astype(F32)
    r_all[y] = total
    r_copies = to_dp(r_all, r_send, r_recv)

    def sent_step(step, carry):
        to, copy, rest_copy = block_copy(step)

        @pl.when(to != seq)
        def done():
            copy.wait_send()
            rest_copy.wait_send()

        return carry

    lax.fori_loop(0, owners, sent_step, 0)
    pl.when(seq < last)(up.wait_send)
    pl.when(seq > 0)(down.wait_send)
    for turn in range(X):
        core_copy(turn).wait_send()
        for k in range(1, Y):
            y_copy(turn, k).wait_send()
        for k in range(1 if turn == X - 1 else 0, Z):
            w_copy(turn, k).wait_send()
    for turn in range(X - 1):
        x_copy(turn).wait_send()
    for copy in s_copies:
        copy.wait_recv()
    gradient_ref[:, 0:half_width] = (y_all[0] + y_all[1]) + (y_all[2] + y_all[3])
    for copy in r_copies:
        copy.wait_recv()
    for k in range(Y):
        at = half_width + k * strip_width
        gradient_ref[:, at : at + strip_width] = r_all[k]
    for copy in z_copies + s_copies + r_copies:
        copy.wait_send()


def place_kernel(processed_ref, gradient_ref, processed_out, gradient_out):
    processed_out[0] = processed_ref[...]
    gradient_out[...] = gradient_ref[...]


def shards(
    grid_fields, mesh_latent, edge_source, edge_target, edge_count, edge_bias, encoder_proj,
    norm_gain, processor_proj, offset_bias, windows, output_proj, cotangent,
):
    shard_count = lax.axis_size("seq")
    device = lax.axis_index("seq")
    rows, width = mesh_latent.shape
    heads = offset_bias.shape[0]
    reach = (offset_bias.shape[1] - 1) // 2
    channels, points = grid_fields.shape[1:]
    capacity = edge_source.shape[2]
    main = channels // 16 * 16
    chips = shard_count // CORES
    strip_width = width // 2 // Y
    dma = pltpu.SemaphoreType.DMA
    hbm = pl.BlockSpec(memory_space=pltpu.HBM)
    processed, gradient = pl.pallas_call(
        layer_kernel,
        out_shape=(
            jax.ShapeDtypeStruct((rows, width), BF16),
            jax.ShapeDtypeStruct((16, width), F32),
        ),
        in_specs=[pl.BlockSpec(memory_space=pltpu.SMEM)] * 2 + [vmem()] * 8 + [hbm] * 3,
        out_specs=(vmem(), vmem()),
        scratch_shapes=[
            pltpu.VMEM((points, 128), F32),
            pltpu.VMEM((128, 128), F32),
            pltpu.VMEM((shard_count, main, capacity), BF16),
            pltpu.VMEM((shard_count, main, capacity), BF16),
            pltpu.VMEM((shard_count, channels - main, capacity), F32),
            pltpu.VMEM((shard_count, channels - main, capacity), F32),
            pltpu.VMEM((width, rows), BF16),
            pltpu.VMEM((2 * width, 128), BF16),
            pltpu.VMEM((shard_count, capacity), jnp.int32),
            pltpu.VMEM((chips, capacity), jnp.int32),
            pltpu.VMEM((2, chips, capacity), F32),
            pltpu.VMEM((width, rows), F32),
            pltpu.VMEM((heads, rows), F32),
            pltpu.VMEM((heads, rows), F32),
            dma((shard_count,)),
            dma((shard_count,)),
            dma((shard_count,)),
            dma((shard_count,)),
            pltpu.VMEM((width, 3 * width), BF16),
            pltpu.VMEM((width, width), BF16),
            pltpu.VMEM((1, rows, width), BF16),
            dma((3,)),
            pltpu.VMEM((rows, width), F32),
            pltpu.VMEM((rows + 2 * reach, width), BF16),
            pltpu.VMEM((rows + 2 * reach, 3 * width), BF16),
            pltpu.VMEM((heads, 3 * reach), F32),
            pltpu.VMEM((2, heads // 2, 3 * reach, 2 * reach), F32),
            pltpu.VMEM((width, rows), BF16),
            pltpu.VMEM((rows, width), BF16),
            dma((2,)),
            dma((2,)),
            pltpu.VMEM((X, Z, CORES, 16, width), BF16),
            pltpu.VMEM((X, Z, 16, width), BF16),
            pltpu.VMEM((X, Z, 16, width), BF16),
            pltpu.VMEM((Y - 1, X, Z, 16, strip_width), BF16),
            pltpu.VMEM((X, Z, 16, strip_width), BF16),
            pltpu.VMEM((X, Z, 16, strip_width), BF16),
            pltpu.VMEM((Y, 16, strip_width), F32),
            pltpu.VMEM((X - 1, Z, 16, width // 2), BF16),
            pltpu.VMEM((Z, 16, width // 2), BF16),
            pltpu.VMEM((Z - 1, 16, width // 2), BF16),
            pltpu.VMEM((Y, 16, width // 2), F32),
            dma((X,)),
            dma((X,)),
            dma((Y - 1, X)),
            dma((Y - 1, X)),
            dma((X, Z)),
            dma((X, Z)),
            dma((Y - 1,)),
            dma((Y - 1,)),
            dma((X - 1,)),
            dma((X - 1,)),
            dma((Z - 1,)),
            dma((Z - 1,)),
            dma((Y - 1,)),
            dma((Y - 1,)),
        ],
        compiler_params=pltpu.CompilerParams(
            vmem_limit_bytes=VMEM_LIMIT, collective_id=2, has_side_effects=True
        ),
        name="layer",
    )(
        edge_source[0], windows, grid_fields, edge_target[0], edge_count, edge_bias[0], mesh_latent,
        encoder_proj, norm_gain[None], offset_bias, processor_proj, output_proj, cotangent,
    )

    return pl.pallas_call(
        place_kernel,
        out_shape=(
            jax.ShapeDtypeStruct((1, rows, width), BF16),
            jax.ShapeDtypeStruct((16, width), F32),
        ),
        in_specs=[vmem(), vmem()],
        out_specs=(vmem(), vmem()),
        name="place",
    )(processed, gradient)


def solution(mesh):
    in_specs = (
        P("dp", None, "seq"),
        P("seq", None),
        P("seq", None, None),
        P("seq", None, None),
        P(),
        P("seq", None, None),
        P(),
        P(),
        P(),
        P(),
        P(),
        P(),
        P("dp", "seq", None),
    )
    out_specs = (P("dp", "seq", None), P("seq", None))
    return jax.shard_map(shards, mesh=mesh, in_specs=in_specs, out_specs=out_specs, check_vma=False)
```
